32 devices in a mesh: parts: 2 (over y), cols: 4 (over z), rows: 2 (over x), rep: 2 (over core).
Axes of the slice: x: 2, y: 2, z: 4, core: 2. Of those that a mesh axis runs over, the one named last changes fastest.
Arguments:
- sources: float32 [4096, 64], P(('parts', 'rows')), parts along dimension 0, may hold values from -11 to 11
- source_mass: float32 [4096], P(('parts', 'rows')), parts along dimension 0, may hold values from 0.2 to 5
- targets: float32 [4096, 64], P(('parts', 'cols', 'rep')), parts along dimension 0, may hold values from -6 to 6
- target_mass: float32 [4096], P(('parts', 'cols', 'rep')), parts along dimension 0, may hold values from 0.2 to 5
- fate_panel: float32 [4096, 64], P(('parts', 'cols', 'rep')), parts along dimension 0, may hold values from 0 to 1
Outputs:
- f_pot: float32 [4096], P(('parts', 'rows')), parts along dimension 0
- g_pot: float32 [4096], P(('parts', 'cols', 'rep')), parts along dimension 0
- fate_rows: float32 [4096, 64], P(('parts', 'rows', 'cols', 'rep')), parts along dimension 0
The draws below stay inside these ranges and needn't reach their ends.
There are 2 independent parts, one for each index of `parts`. The reference program is written for one: setup_inputs(seed, part) draws one part's arguments, and reference() takes and returns one part's arrays. A program takes and returns all parts, laid end to end along the dimension named above; each array names one. Nothing has to cross between parts.
All inputs are finite; a program needn't handle non-finite values.
Results may differ from the reference program's by a relative error of at most 0.0003.
Values sent between devices are 32-bit elements; how exact they have to be, the bound alone decides.
A program may use at most 64 MiB of HBM per device.

```python
import math
import jax
import jax.numpy as jnp
from jax import lax

DIM = 64
FATES = 64
ITERS = 8
NS = 2048
NT = 2048


def draw_sources(key, part):
    key_base = jax.random.fold_in(key, 0)
    return jnp.clip(jax.random.normal(key_base, (NS, DIM), jnp.float32), -6.0, 6.0)


def level_of(rng, shape, pieces, smallest, largest):
    gain = 1.0
    for position, shards_of in pieces:
        draws = jax.random.uniform(jax.random.fold_in(jax.random.fold_in(rng, 6), position), (shards_of,), jnp.float32, smallest / len(pieces), largest / len(pieces))
        gain = gain * jnp.repeat(jnp.exp(draws), shape[position] // shards_of).reshape((-1,) + (1,) * (len(shape) - 1 - position))
    return gain


def centred(key, shape, scale, reach, cuts=(), kind=jnp.bfloat16):
    result = jax.random.normal(key, shape, jnp.float32) * scale
    if len(cuts) > 0:
        result = level_of(key, shape, cuts, -0.22, 0.18) * result
    return jnp.clip(result, min=-reach, max=reach).astype(kind)


def setup_inputs(seed: int = 0, part: int = 0) -> dict:
    key_of = jax.random.split(jax.random.key(seed), 6)
    part_splits = jax.random.split(jax.random.fold_in(key_of[5], part), 6)
    return {
        "sources": draw_sources(jax.random.fold_in(jax.random.fold_in(key_of[5], part), 71), part),
        "source_mass": jnp.clip(jnp.exp(math.log(5.0) - 3.218876 * jax.random.uniform(part_splits[1], (NS,), jnp.float32) ** level_of(part_splits[1], (NS,), ((0, 2),), -0.2, 0.2)), 0.2, 5.0),
        "targets": centred(part_splits[2], (NT, DIM), 1.0, 6.0, ((0, 8),), jnp.float32),
        "target_mass": jnp.clip(jnp.exp(math.log(5.0) - 3.218876 * jax.random.uniform(part_splits[3], (NT,), jnp.float32) ** level_of(part_splits[3], (NT,), ((0, 8),), -0.2, 0.2)), 0.2, 5.0),
        "fate_panel": jnp.clip(1.0 * jax.random.uniform(part_splits[4], (NT, FATES), jnp.float32) ** level_of(part_splits[4], (NT, FATES), ((0, 8),), -0.2, 0.2), 0.0, 1.0),
    }


entropic = 0.1
relaxed = 1.0 / 1.1


def pair_cost(lhs_rows, rhs_rows):
    lhs_sq = jnp.sum(lhs_rows * lhs_rows, axis=1)
    rhs_sq = jnp.sum(rhs_rows * rhs_rows, axis=1)
    products = lax.dot_general(lhs_rows, rhs_rows, (((1,), (1,)), ((), ())), precision=lax.Precision.HIGHEST, preferred_element_type=jnp.float32)
    return (lhs_sq[:, None] + rhs_sq[None, :] - 2.0 * products) / DIM


def reference(sources, source_mass, targets, target_mass, fate_panel):
    log_a = jnp.log(source_mass / NS)
    log_b = jnp.log(target_mass / NT)
    row_size = math.gcd(NS, 512)
    col_size = math.gcd(NT, 512)
    src_blocks = sources.reshape(NS // row_size, row_size, DIM)
    tgt_blocks = targets.reshape(NT // col_size, col_size, DIM)

    def row_lse(g_pot):
        def single_block(src_block):
            scores = log_b[None, :] + (g_pot[None, :] - pair_cost(src_block, targets)) / entropic
            highest = jnp.max(scores, axis=1)
            totals = jnp.sum(jnp.exp(scores - highest[:, None]), axis=1)
            return -relaxed * entropic * (highest + jnp.log(totals))
        return lax.map(single_block, src_blocks).reshape(NS)

    def col_lse(f_pot):
        def single_block(tgt_block):
            scores = log_a[:, None] + (f_pot[:, None] - pair_cost(sources, tgt_block)) / entropic
            highest = jnp.max(scores, axis=0)
            totals = jnp.sum(jnp.exp(scores - highest[None, :]), axis=0)
            return -relaxed * entropic * (highest + jnp.log(totals))
        return lax.map(single_block, tgt_blocks).reshape(NT)

    g_pot = jnp.zeros((NT,), jnp.float32)
    f_pot = jnp.zeros((NS,), jnp.float32)
    for iteration in range(ITERS):
        f_pot = row_lse(g_pot)
        g_pot = col_lse(f_pot)

    def fate_block(src_block):
        scores = log_b[None, :] + (g_pot[None, :] - pair_cost(src_block, targets)) / entropic
        highest = jnp.max(scores, axis=1)
        weights = jnp.exp(scores - highest[:, None])
        totals = jnp.sum(weights, axis=1)
        weighted = jnp.dot(weights, fate_panel, precision=lax.Precision.HIGHEST, preferred_element_type=jnp.float32)
        return weighted / totals[:, None]

    fate_rows = lax.map(fate_block, src_blocks).reshape(NS, FATES)
    return (f_pot, g_pot, fate_rows)
```

```python
import functools
import math

import jax
import jax.numpy as jnp
from jax import lax
from jax.experimental import pallas as pl
from jax.experimental.pallas import tpu as pltpu
from jax.sharding import PartitionSpec as P

ITERS = 8
LANES = 128
CHUNK = 8
entropic = 0.1
relaxed = 1.0 / 1.1
HIGHEST = lax.Precision.HIGHEST
MESH = pl.DeviceIdType.MESH


def peak_total(x):
    peak = jnp.max(x, axis=0)
    return peak, jnp.sum(jnp.exp2(x - peak[None]), axis=0)


def kernel(
    sizes, src_ref, smass_ref, tgt_ref, tmass_ref, fate_ref,
    f_ref, g_ref, out_ref,
    tt, ft, scores, log_b, g_scaled, log_a, f_scaled, row_peak, row_total, parts, f_parts,
    tt_send, tt_recv, fwd_send, fwd_recv, ft_send, ft_recv, ex_send, ex_recv, f_send, f_recv,
):
    X, C, R, src_count, tgt_count, dim, fates = sizes
    rows = src_count // R
    own = src_count // (C * R)
    blocks = C * R * tgt_count // LANES
    chunks = blocks // CHUNK
    per = tgt_count // LANES
    groups = rows // 8
    peers = X * R
    x_id, c_id, r_id = lax.axis_index("rows"), lax.axis_index("cols"), lax.axis_index("rep")
    me = x_id * R + r_id
    all_sources, all_targets = src_count * X, tgt_count * C * R
    unit = math.log2(math.e) / (dim * entropic)

    def peer(step):
        other = lax.rem(me + step, peers)
        return {"rows": other // R, "rep": lax.rem(other, R)}

    def col_of(step):
        return lax.rem(c_id + step, C)

    def rep_of(step):
        return lax.rem(r_id + step, R)

    barrier = pltpu.get_barrier_semaphore()
    for step in range(1, peers):
        pl.semaphore_signal(barrier, inc=1, device_id=peer(step), device_id_type=MESH)
    for step in range(1, C):
        for turn in range(R):
            pl.semaphore_signal(
                barrier, inc=1, device_id={"cols": col_of(step), "rep": rep_of(turn)},
                device_id_type=MESH,
            )

    both = jnp.concatenate([tgt_ref[...], fate_ref[...]], axis=1)
    for k in range(per):
        turned = both[k * LANES:(k + 1) * LANES].T
        tt[c_id, r_id, 0:dim, k * LANES:(k + 1) * LANES] = turned[:dim]
        ft[c_id, r_id, :, k * LANES:(k + 1) * LANES] = turned[dim:]
    tt[c_id, r_id, dim:dim + 8, :] = jnp.broadcast_to(
        jnp.log2(tmass_ref[...] / all_targets), (8, tgt_count)
    )

    pl.semaphore_wait(barrier, peers - 1 + (C - 1) * R)

    def tt_copy(step):
        return pltpu.make_async_remote_copy(
            src_ref=tt.at[c_id, r_id], dst_ref=tt.at[c_id, r_id],
            send_sem=tt_send.at[step], recv_sem=tt_recv.at[c_id],
            device_id={"cols": col_of(step)}, device_id_type=MESH,
        )

    def fwd_copy(col, turn):
        return pltpu.make_async_remote_copy(
            src_ref=tt.at[col, r_id], dst_ref=tt.at[col, r_id],
            send_sem=fwd_send.at[col, turn], recv_sem=fwd_recv.at[col, r_id],
            device_id={"rep": rep_of(turn)}, device_id_type=MESH,
        )

    def ft_copy(step, turn):
        return pltpu.make_async_remote_copy(
            src_ref=ft.at[c_id, r_id], dst_ref=ft.at[c_id, r_id],
            send_sem=ft_send.at[step, turn], recv_sem=ft_recv.at[c_id, r_id],
            device_id={"cols": col_of(step), "rep": rep_of(turn)}, device_id_type=MESH,
        )

    def tt_arrived(col):
        pltpu.make_async_remote_copy(
            src_ref=tt.at[col, r_id], dst_ref=tt.at[col, r_id],
            send_sem=tt_send.at[0], recv_sem=tt_recv.at[col],
            device_id={"cols": col}, device_id_type=MESH,
        ).wait_recv()

    def fwd_arrived(col, rep):
        pltpu.make_async_remote_copy(
            src_ref=tt.at[col, rep], dst_ref=tt.at[col, rep],
            send_sem=fwd_send.at[col, 0], recv_sem=fwd_recv.at[col, rep],
            device_id={"rep": rep}, device_id_type=MESH,
        ).wait_recv()

    def ft_arrived(col, rep):
        pltpu.make_async_remote_copy(
            src_ref=ft.at[col, rep], dst_ref=ft.at[col, rep],
            send_sem=ft_send.at[0, 0], recv_sem=ft_recv.at[col, rep],
            device_id={"cols": col, "rep": rep}, device_id_type=MESH,
        ).wait_recv()

    for step in range(1, C):
        tt_copy(step).start()
    for turn in range(1, R):
        fwd_copy(c_id, turn).start()
    for step in list(range(1, C)) + [0]:
        for turn in range(R):
            if step or turn:
                ft_copy(step, turn).start()

    first = pl.multiple_of(r_id * rows, rows)
    first_own = pl.multiple_of((c_id * R + r_id) * own, own)
    mine = jnp.concatenate([src_ref[pl.ds(first, rows), :], src_ref[pl.ds(first_own, own), :]], axis=0)
    src_sq = jnp.sum(mine * mine, axis=1, keepdims=True) * unit
    mine = mine * (2.0 * unit)

    def fill(col, rep):
        block = tt[col, rep, 0:dim, :]
        products = jnp.dot(mine, block, precision=HIGHEST, preferred_element_type=jnp.float32)
        values = products - (src_sq + jnp.sum(block * block, axis=0, keepdims=True) * unit)
        for k in range(per):
            at = (col * R + rep) * per + k
            scores[at] = values[:, k * LANES:(k + 1) * LANES]
            level = tt[col, rep, dim:dim + 8, k * LANES:(k + 1) * LANES]
            log_b[at] = level
            g_scaled[at] = level

    fill(c_id, r_id)
    for k in range(rows // LANES):
        level = jnp.log2(smass_ref[r_id, k:k + 1, :] / all_sources)
        log_a[k * LANES:(k + 1) * LANES, :] = jnp.broadcast_to(level, (LANES, LANES)).T
    for turn in range(1, R):
        fwd_arrived(c_id, rep_of(turn))
        fill(c_id, rep_of(turn))
    for step in range(1, C):
        tt_arrived(col_of(step))
        for turn in range(1, R):
            fwd_copy(col_of(step), turn).start()
        fill(col_of(step), r_id)
    for step in range(1, C):
        for turn in range(1, R):
            fwd_arrived(col_of(step), rep_of(turn))
            fill(col_of(step), rep_of(turn))

    def row_chunk(chunk):
        def row_group(group, carry):
            at = pl.multiple_of(group * 8, 8)
            base = chunk * CHUNK
            x = scores[pl.ds(base, CHUNK), pl.ds(at, 8), :] + g_scaled[pl.ds(base, CHUNK)]
            peak, total = peak_total(x)
            row_peak[chunk, pl.ds(at, 8), :] = peak
            row_total[chunk, pl.ds(at, 8), :] = total
            return carry

        lax.fori_loop(0, groups, row_group, 0, unroll=4)

    def row_finish():
        def some(k, carry):
            at = pl.multiple_of(k * 64, 64)
            peaks = row_peak[:, pl.ds(at, 64), :]
            top = jnp.max(jnp.max(peaks, axis=0), axis=1, keepdims=True)
            totals = jnp.sum(row_total[:, pl.ds(at, 64), :] * jnp.exp2(peaks - top[None]), axis=0)
            level = top + jnp.log2(jnp.sum(totals, axis=1, keepdims=True))
            f_scaled[pl.ds(at, 64), :] = log_a[pl.ds(at, 64), :] - relaxed * level
            return carry

        lax.fori_loop(0, rows // 64, some, 0, unroll=2)

    def col_block(block):
        peaks, totals = [], []
        for q in range(rows // LANES):
            at = slice(q * LANES, (q + 1) * LANES)
            x = (scores[block, at, :] + f_scaled[at, :]).reshape(LANES // 8, 8, LANES)
            peak, total = peak_total(x)
            peaks.append(peak)
            totals.append(total)
        top = jnp.max(functools.reduce(jnp.maximum, peaks), axis=0, keepdims=True)
        whole = sum(t * jnp.exp2(p - top) for p, t in zip(peaks, totals))
        return top + jnp.log2(jnp.sum(whole, axis=0, keepdims=True))

    def ex_copy(slot, chunk, step):
        return pltpu.make_async_remote_copy(
            src_ref=parts.at[slot, chunk, me], dst_ref=parts.at[slot, chunk, me],
            send_sem=ex_send.at[slot, chunk, step], recv_sem=ex_recv.at[slot, chunk, me],
            device_id=peer(step), device_id_type=MESH,
        )

    def ex_arrived(slot, chunk, step):
        other = lax.rem(me + step, peers)
        pltpu.make_async_remote_copy(
            src_ref=parts.at[slot, chunk, other], dst_ref=parts.at[slot, chunk, other],
            send_sem=ex_send.at[slot, chunk, 0], recv_sem=ex_recv.at[slot, chunk, other],
            device_id=peer(step), device_id_type=MESH,
        ).wait_recv()

    for chunk in range(chunks):
        row_chunk(chunk)

    def iteration(it, carry):
        slot = lax.rem(it, 2)
        row_finish()
        for chunk in range(chunks):
            for j in range(CHUNK):
                parts[slot, chunk, me, j:j + 1, :] = col_block(chunk * CHUNK + j)
            for step in range(1, peers):
                ex_copy(slot, chunk, step).start()
        for chunk in range(chunks):
            for step in range(1, peers):
                ex_arrived(slot, chunk, step)
            peak, total = peak_total(parts[slot, chunk])
            level = -relaxed * (peak + jnp.log2(total))
            for j in range(CHUNK):
                g_scaled[chunk * CHUNK + j] = (
                    jnp.broadcast_to(level[j:j + 1, :], (8, LANES)) + log_b[chunk * CHUNK + j]
                )
            row_chunk(chunk)
        for chunk in range(chunks):
            for step in range(1, peers):
                ex_copy(slot, chunk, step).wait_send()
        return carry

    lax.fori_loop(0, ITERS, iteration, 0)

    back = entropic * math.log(2.0)
    for k in range(rows // LANES):
        at = slice(k * LANES, (k + 1) * LANES)
        turned = ((f_scaled[at, :] - log_a[at, :]) * back).T
        f_parts[r_id, k:k + 1, :] = turned[0:1, :]

    def f_copy(turn):
        return pltpu.make_async_remote_copy(
            src_ref=f_parts.at[r_id], dst_ref=f_parts.at[r_id],
            send_sem=f_send.at[turn], recv_sem=f_recv.at[r_id],
            device_id={"rep": rep_of(turn)}, device_id_type=MESH,
        )

    for turn in range(1, R):
        f_copy(turn).start()
    for k in range(per):
        at = (c_id * R + r_id) * per + k
        g_ref[k:k + 1, :] = ((g_scaled[at] - log_b[at]) * back)[0:1, :]

    def own_scores(block):
        return scores[block, rows:rows + own, :].reshape(own // 8, 8, LANES) + g_scaled[block][None]

    def own_peak(block, peak):
        return jnp.maximum(peak, own_scores(block))

    peak = lax.fori_loop(1, blocks, own_peak, own_scores(0), unroll=5)
    top = jnp.max(peak, axis=2, keepdims=True)
    for step in range(C):
        for turn in range(R):
            if step or turn:
                ft_arrived(col_of(step), rep_of(turn))

    def fate_block(block, carry):
        total, weighted = carry
        pieces = [jnp.exp2(own_scores(block * per + k) - top) for k in range(per)]
        total = total + sum(pieces)
        weights = jnp.concatenate([p.reshape(own, LANES) for p in pieces], axis=1)
        weighted = weighted + lax.dot_general(
            weights, ft[block // R, lax.rem(block, R)], (((1,), (1,)), ((), ())),
            precision=HIGHEST, preferred_element_type=jnp.float32,
        )
        return total, weighted

    total, weighted = lax.fori_loop(
        0, C * R, fate_block,
        (jnp.zeros((own // 8, 8, LANES), jnp.float32), jnp.zeros((own, fates), jnp.float32)),
    )
    out_ref[...] = weighted / jnp.sum(total.reshape(own, LANES), axis=1, keepdims=True)
    for turn in range(1, R):
        pltpu.make_async_remote_copy(
            src_ref=f_parts.at[rep_of(turn)], dst_ref=f_parts.at[rep_of(turn)],
            send_sem=f_send.at[0], recv_sem=f_recv.at[rep_of(turn)],
            device_id={"rep": rep_of(turn)}, device_id_type=MESH,
        ).wait_recv()
    f_ref[...] = f_parts[...]

    for turn in range(1, R):
        f_copy(turn).wait_send()
        for step in range(C):
            fwd_copy(col_of(step), turn).wait_send()
    for step in range(1, C):
        tt_copy(step).wait_send()
    for step in range(C):
        for turn in range(R):
            if step or turn:
                ft_copy(step, turn).wait_send()


def solution(mesh):
    X, C, R = mesh.shape["rows"], mesh.shape["cols"], mesh.shape["rep"]

    def body(sources, source_mass, targets, target_mass, fate_panel):
        src_count, dim = sources.shape
        tgt_count, fates = fate_panel.shape
        rows, own = src_count // R, src_count // (C * R)
        blocks = C * R * tgt_count // LANES
        chunks = blocks // CHUNK
        peers = X * R
        vmem = pl.BlockSpec(memory_space=pltpu.VMEM)
        dma = pltpu.SemaphoreType.DMA
        f32 = jnp.float32
        f_pot, g_pot, fate_rows = pl.pallas_call(
            functools.partial(kernel, (X, C, R, src_count, tgt_count, dim, fates)),
            out_shape=(
                jax.ShapeDtypeStruct((R, rows // LANES, LANES), f32),
                jax.ShapeDtypeStruct((tgt_count // LANES, LANES), f32),
                jax.ShapeDtypeStruct((own, fates), f32),
            ),
            in_specs=[vmem] * 5,
            out_specs=(vmem,) * 3,
            scratch_shapes=[
                pltpu.VMEM((C, R, dim + 8, tgt_count), f32),
                pltpu.VMEM((C, R, fates, tgt_count), f32),
                pltpu.VMEM((blocks, rows + own, LANES), f32),
                pltpu.VMEM((blocks, 8, LANES), f32),
                pltpu.VMEM((blocks, 8, LANES), f32),
                pltpu.VMEM((rows, LANES), f32),
                pltpu.VMEM((rows, LANES), f32),
                pltpu.VMEM((chunks, rows, LANES), f32),
                pltpu.VMEM((chunks, rows, LANES), f32),
                pltpu.VMEM((2, chunks, peers, CHUNK, LANES), f32),
                pltpu.VMEM((R, rows // LANES, LANES), f32),
                dma((C,)), dma((C,)),
                dma((C, R)), dma((C, R)),
                dma((C, R)), dma((C, R)),
                dma((2, chunks, peers)), dma((2, chunks, peers)),
                dma((R,)), dma((R,)),
            ],
            compiler_params=pltpu.CompilerParams(
                collective_id=0, has_side_effects=True, vmem_limit_bytes=48 * 2**20
            ),
            name="transport",
        )(
            sources,
            source_mass.reshape(R, rows // LANES, LANES),
            targets,
            target_mass.reshape(1, tgt_count),
            fate_panel,
        )
        return f_pot.reshape(src_count), g_pot.reshape(tgt_count), fate_rows

    in_specs = (
        P(("parts", "rows"), None),
        P(("parts", "rows")),
        P(("parts", "cols", "rep"), None),
        P(("parts", "cols", "rep")),
        P(("parts", "cols", "rep"), None),
    )
    out_specs = (
        P(("parts", "rows")),
        P(("parts", "cols", "rep")),
        P(("parts", "rows", "cols", "rep"), None),
    )
    return jax.shard_map(body, mesh=mesh, in_specs=in_specs, out_specs=out_specs, check_vma=False)
```

```python
import functools
import math

import jax
import jax.numpy as jnp
from jax import lax
from jax.experimental import pallas as pl
from jax.experimental.pallas import tpu as pltpu
from jax.sharding import PartitionSpec as P

ITERS = 8
LANES = 128
CHUNK = 8
entropic = 0.1
relaxed = 1.0 / 1.1
MESH = pl.DeviceIdType.MESH


def split(x, pieces):
    out = []
    for k in range(pieces):
        out.append(x.astype(jnp.bfloat16).astype(jnp.float32))
        x = x - out[-1]
    return out


def peak_total(x):
    peak = jnp.max(x, axis=0)
    return peak, jnp.sum(jnp.exp2(x - peak[None]), axis=0)


def kernel(
    sizes, src_ref, smass_ref, tgt_ref, tmass_ref, fate_ref,
    f_ref, g_ref, out_ref,
    tt, ft, scores, log_b, g_scaled, log_a, f_scaled, row_peak, row_total, parts, f_parts,
    lhs, src_level,
    tt_send, tt_recv, fwd_send, fwd_recv, ft_send, ft_recv, ex_send, ex_recv, f_send, f_recv,
):
    X, C, R, src_count, tgt_count, dim, fates = sizes
    rows = src_count // R
    own = src_count // (C * R)
    blocks = C * R * tgt_count // LANES
    chunks = blocks // CHUNK
    per = tgt_count // LANES
    groups = rows // 8
    peers = X * R
    x_id, c_id, r_id = lax.axis_index("rows"), lax.axis_index("cols"), lax.axis_index("rep")
    me = x_id * R + r_id
    all_sources, all_targets = src_count * X, tgt_count * C * R
    unit = math.log2(math.e) / (dim * entropic)

    def peer(step):
        other = lax.rem(me + step, peers)
        return {"rows": other // R, "rep": lax.rem(other, R)}

    def col_of(step):
        return lax.rem(c_id + step, C)

    def rep_of(step):
        return lax.rem(r_id + step, R)

    barrier = pltpu.get_barrier_semaphore()
    for step in range(1, peers):
        pl.semaphore_signal(barrier, inc=1, device_id=peer(step), device_id_type=MESH)
    for step in range(1, C):
        for turn in range(R):
            pl.semaphore_signal(
                barrier, inc=1, device_id={"cols": col_of(step), "rep": rep_of(turn)},
                device_id_type=MESH,
            )

    tt[c_id, r_id, 0:dim, :] = tgt_ref[...]
    ft[c_id, r_id, :, :] = fate_ref[...]
    tt[c_id, r_id, dim:dim + 8, :] = jnp.broadcast_to(
        jnp.log2(tmass_ref[...] / all_targets), (8, tgt_count)
    )

    pl.semaphore_wait(barrier, peers - 1 + (C - 1) * R)

    def tt_copy(step):
        return pltpu.make_async_remote_copy(
            src_ref=tt.at[c_id, r_id], dst_ref=tt.at[c_id, r_id],
            send_sem=tt_send.at[step], recv_sem=tt_recv.at[c_id],
            device_id={"cols": col_of(step)}, device_id_type=MESH,
        )

    def fwd_copy(col, turn):
        return pltpu.make_async_remote_copy(
            src_ref=tt.at[col, r_id], dst_ref=tt.at[col, r_id],
            send_sem=fwd_send.at[col, turn], recv_sem=fwd_recv.at[col, r_id],
            device_id={"rep": rep_of(turn)}, device_id_type=MESH,
        )

    def ft_copy(step, turn):
        return pltpu.make_async_remote_copy(
            src_ref=ft.at[c_id, r_id], dst_ref=ft.at[c_id, r_id],
            send_sem=ft_send.at[step, turn], recv_sem=ft_recv.at[c_id, r_id],
            device_id={"cols": col_of(step), "rep": rep_of(turn)}, device_id_type=MESH,
        )

    def tt_arrived(col):
        pltpu.make_async_remote_copy(
            src_ref=tt.at[col, r_id], dst_ref=tt.at[col, r_id],
            send_sem=tt_send.at[0], recv_sem=tt_recv.at[col],
            device_id={"cols": col}, device_id_type=MESH,
        ).wait_recv()

    def fwd_arrived(col, rep):
        pltpu.make_async_remote_copy(
            src_ref=tt.at[col, rep], dst_ref=tt.at[col, rep],
            send_sem=fwd_send.at[col, 0], recv_sem=fwd_recv.at[col, rep],
            device_id={"rep": rep}, device_id_type=MESH,
        ).wait_recv()

    def ft_arrived(col, rep):
        pltpu.make_async_remote_copy(
            src_ref=ft.at[col, rep], dst_ref=ft.at[col, rep],
            send_sem=ft_send.at[0, 0], recv_sem=ft_recv.at[col, rep],
            device_id={"cols": col, "rep": rep}, device_id_type=MESH,
        ).wait_recv()

    for step in range(1, C):
        tt_copy(step).start()
    for turn in range(1, R):
        fwd_copy(c_id, turn).start()
    for step in list(range(1, C)) + [0]:
        for turn in range(R):
            if step or turn:
                ft_copy(step, turn).start()

    first = pl.multiple_of(r_id * rows, rows)
    first_own = pl.multiple_of((c_id * R + r_id) * own, own)
    mine = jnp.concatenate([src_ref[pl.ds(first, rows), :], src_ref[pl.ds(first_own, own), :]], axis=0)
    src_level[...] = jnp.broadcast_to(
        jnp.sum(mine * mine, axis=1, keepdims=True) * unit, src_level.shape
    )
    a, b, c = split(mine * (2.0 * unit), 3)
    lhs[...] = jnp.concatenate([a, a, b, a, c, b], axis=1).astype(jnp.bfloat16)

    def fill(col, rep):
        block = tt[col, rep, 0:dim, :]
        a, b, c = [p.astype(jnp.bfloat16) for p in split(block, 3)]
        rhs = jnp.concatenate([a, b, a, c, a, b], axis=0)
        products = jnp.dot(lhs[...], rhs, preferred_element_type=jnp.float32)
        tgt_level = jnp.sum(block * block, axis=0, keepdims=True) * unit
        for k in range(per):
            at = (col * R + rep) * per + k
            lanes = slice(k * LANES, (k + 1) * LANES)
            scores[at] = products[:, lanes] - (src_level[...] + tgt_level[:, lanes])
            level = tt[col, rep, dim:dim + 8, k * LANES:(k + 1) * LANES]
            log_b[at] = level
            g_scaled[at] = level

    fill(c_id, r_id)
    for k in range(rows // LANES):
        level = jnp.log2(smass_ref[r_id, k:k + 1, :] / all_sources)
        log_a[k * LANES:(k + 1) * LANES, :] = jnp.broadcast_to(level, (LANES, LANES)).T
    for turn in range(1, R):
        fwd_arrived(c_id, rep_of(turn))
        fill(c_id, rep_of(turn))
    for step in range(1, C):
        tt_arrived(col_of(step))
        for turn in range(1, R):
            fwd_copy(col_of(step), turn).start()
        fill(col_of(step), r_id)
    for step in range(1, C):
        for turn in range(1, R):
            fwd_arrived(col_of(step), rep_of(turn))
            fill(col_of(step), rep_of(turn))

    def row_chunk(chunk):
        def row_group(group, carry):
            at = pl.multiple_of(group * 8, 8)
            base = chunk * CHUNK
            x = scores[pl.ds(base, CHUNK), pl.ds(at, 8), :] + g_scaled[pl.ds(base, CHUNK)]
            peak, total = peak_total(x)
            row_peak[chunk, pl.ds(at, 8), :] = peak
            row_total[chunk, pl.ds(at, 8), :] = total
            return carry

        lax.fori_loop(0, groups, row_group, 0, unroll=8)

    def row_finish():
        peaks = row_peak[...]
        top = jnp.max(jnp.max(peaks, axis=0), axis=1, keepdims=True)
        totals = jnp.sum(row_total[...] * jnp.exp2(peaks - top[None]), axis=0)
        level = top + jnp.log2(jnp.sum(totals, axis=1, keepdims=True))
        f_scaled[...] = log_a[...] - relaxed * level

    def col_block(block):
        peaks, totals = [], []
        for q in range(rows // LANES):
            at = slice(q * LANES, (q + 1) * LANES)
            x = (scores[block, at, :] + f_scaled[at, :]).reshape(LANES // 8, 8, LANES)
            peak, total = peak_total(x)
            peaks.append(peak)
            totals.append(total)
        top = jnp.max(functools.reduce(jnp.maximum, peaks), axis=0, keepdims=True)
        whole = sum(t * jnp.exp2(p - top) for p, t in zip(peaks, totals))
        return top + jnp.log2(jnp.sum(whole, axis=0, keepdims=True))

    def ex_copy(slot, chunk, step):
        return pltpu.make_async_remote_copy(
            src_ref=parts.at[slot, chunk, me], dst_ref=parts.at[slot, chunk, me],
            send_sem=ex_send.at[slot, chunk, step], recv_sem=ex_recv.at[slot, chunk, me],
            device_id=peer(step), device_id_type=MESH,
        )

    def ex_arrived(slot, chunk, step):
        other = lax.rem(me + step, peers)
        pltpu.make_async_remote_copy(
            src_ref=parts.at[slot, chunk, other], dst_ref=parts.at[slot, chunk, other],
            send_sem=ex_send.at[slot, chunk, 0], recv_sem=ex_recv.at[slot, chunk, other],
            device_id=peer(step), device_id_type=MESH,
        ).wait_recv()

    for chunk in range(chunks):
        row_chunk(chunk)

    def iteration(it, carry):
        slot = lax.rem(it, 2)
        row_finish()
        for chunk in range(chunks):
            for j in range(CHUNK):
                parts[slot, chunk, me, j:j + 1, :] = col_block(chunk * CHUNK + j)
            for step in range(1, peers):
                ex_copy(slot, chunk, step).start()
        for chunk in range(chunks):
            for step in range(1, peers):
                ex_arrived(slot, chunk, step)
            peak, total = peak_total(parts[slot, chunk])
            level = -relaxed * (peak + jnp.log2(total))
            for j in range(CHUNK):
                g_scaled[chunk * CHUNK + j] = (
                    jnp.broadcast_to(level[j:j + 1, :], (8, LANES)) + log_b[chunk * CHUNK + j]
                )
            row_chunk(chunk)
        for chunk in range(chunks):
            for step in range(1, peers):
                ex_copy(slot, chunk, step).wait_send()
        return carry

    lax.fori_loop(0, ITERS, iteration, 0)

    back = entropic * math.log(2.0)
    for k in range(rows // LANES):
        at = slice(k * LANES, (k + 1) * LANES)
        turned = ((f_scaled[at, :] - log_a[at, :]) * back).T
        f_parts[r_id, k:k + 1, :] = turned[0:1, :]

    def f_copy(turn):
        return pltpu.make_async_remote_copy(
            src_ref=f_parts.at[r_id], dst_ref=f_parts.at[r_id],
            send_sem=f_send.at[turn], recv_sem=f_recv.at[r_id],
            device_id={"rep": rep_of(turn)}, device_id_type=MESH,
        )

    for turn in range(1, R):
        f_copy(turn).start()
    for k in range(per):
        at = (c_id * R + r_id) * per + k
        g_ref[k:k + 1, :] = ((g_scaled[at] - log_b[at]) * back)[0:1, :]

    def own_scores(block):
        return scores[block, rows:rows + own, :].reshape(own // 8, 8, LANES) + g_scaled[block][None]

    def own_peak(block, peak):
        return jnp.maximum(peak, own_scores(block))

    peak = lax.fori_loop(1, blocks, own_peak, own_scores(0), unroll=5)
    top = jnp.max(peak, axis=2, keepdims=True)
    for step in range(C):
        for turn in range(R):
            if step or turn:
                ft_arrived(col_of(step), rep_of(turn))

    def across(left, right):
        return lax.dot_general(
            left, right, (((1,), (1,)), ((), ())), preferred_element_type=jnp.float32
        )

    def fate_block(block, carry):
        total, weighted = carry
        pieces = [jnp.exp2(own_scores(block * per + k) - top) for k in range(per)]
        total = total + sum(pieces)
        weights = jnp.concatenate([p.reshape(own, LANES) for p in pieces], axis=1)
        high, low = [p.astype(jnp.bfloat16) for p in split(weights, 2)]
        panel = [p.astype(jnp.bfloat16) for p in split(ft[block // R, lax.rem(block, R)], 2)]
        return total, weighted + across(high, jnp.concatenate(panel, axis=0)) + across(
            low, jnp.concatenate([panel[0], jnp.zeros_like(panel[0])], axis=0)
        )

    total, weighted = lax.fori_loop(
        0, C * R, fate_block,
        (jnp.zeros((own // 8, 8, LANES), jnp.float32), jnp.zeros((own, 2 * fates), jnp.float32)),
    )
    weighted = weighted / jnp.sum(total.reshape(own, LANES), axis=1, keepdims=True)
    turned = weighted.T
    out_ref[...] = turned[:fates] + turned[fates:]
    for turn in range(1, R):
        pltpu.make_async_remote_copy(
            src_ref=f_parts.at[rep_of(turn)], dst_ref=f_parts.at[rep_of(turn)],
            send_sem=f_send.at[0], recv_sem=f_recv.at[rep_of(turn)],
            device_id={"rep": rep_of(turn)}, device_id_type=MESH,
        ).wait_recv()
    f_ref[...] = f_parts[...]

    for turn in range(1, R):
        f_copy(turn).wait_send()
        for step in range(C):
            fwd_copy(col_of(step), turn).wait_send()
    for step in range(1, C):
        tt_copy(step).wait_send()
    for step in range(C):
        for turn in range(R):
            if step or turn:
                ft_copy(step, turn).wait_send()


def solution(mesh):
    X, C, R = mesh.shape["rows"], mesh.shape["cols"], mesh.shape["rep"]

    def body(sources, source_mass, targets, target_mass, fate_panel):
        src_count, dim = sources.shape
        tgt_count, fates = fate_panel.shape
        rows, own = src_count // R, src_count // (C * R)
        blocks = C * R * tgt_count // LANES
        chunks = blocks // CHUNK
        peers = X * R
        vmem = pl.BlockSpec(memory_space=pltpu.VMEM)
        dma = pltpu.SemaphoreType.DMA
        f32 = jnp.float32
        f_pot, g_pot, fate_rows = pl.pallas_call(
            functools.partial(kernel, (X, C, R, src_count, tgt_count, dim, fates)),
            out_shape=(
                jax.ShapeDtypeStruct((R, rows // LANES, LANES), f32),
                jax.ShapeDtypeStruct((tgt_count // LANES, LANES), f32),
                jax.ShapeDtypeStruct((fates, own), f32),
            ),
            in_specs=[vmem] * 5,
            out_specs=(vmem,) * 3,
            scratch_shapes=[
                pltpu.VMEM((C, R, dim + 8, tgt_count), f32),
                pltpu.VMEM((C, R, fates, tgt_count), f32),
                pltpu.VMEM((blocks, rows + own, LANES), f32),
                pltpu.VMEM((blocks, 8, LANES), f32),
                pltpu.VMEM((blocks, 8, LANES), f32),
                pltpu.VMEM((rows, LANES), f32),
                pltpu.VMEM((rows, LANES), f32),
                pltpu.VMEM((chunks, rows, LANES), f32),
                pltpu.VMEM((chunks, rows, LANES), f32),
                pltpu.VMEM((2, chunks, peers, CHUNK, LANES), f32),
                pltpu.VMEM((R, rows // LANES, LANES), f32),
                pltpu.VMEM((rows + own, 6 * dim), jnp.bfloat16),
                pltpu.VMEM((rows + own, LANES), f32),
                dma((C,)), dma((C,)),
                dma((C, R)), dma((C, R)),
                dma((C, R)), dma((C, R)),
                dma((2, chunks, peers)), dma((2, chunks, peers)),
                dma((R,)), dma((R,)),
            ],
            compiler_params=pltpu.CompilerParams(
                collective_id=0, has_side_effects=True, vmem_limit_bytes=48 * 2**20
            ),
            name="transport",
        )(
            sources,
            source_mass.reshape(R, rows // LANES, LANES),
            targets.T,
            target_mass.reshape(1, tgt_count),
            fate_panel.T,
        )
        return f_pot.reshape(src_count), g_pot.reshape(tgt_count), fate_rows.T

    in_specs = (
        P(("parts", "rows"), None),
        P(("parts", "rows")),
        P(("parts", "cols", "rep"), None),
        P(("parts", "cols", "rep")),
        P(("parts", "cols", "rep"), None),
    )
    out_specs = (
        P(("parts", "rows")),
        P(("parts", "cols", "rep")),
        P(("parts", "rows", "cols", "rep"), None),
    )
    return jax.shard_map(body, mesh=mesh, in_specs=in_specs, out_specs=out_specs, check_vma=False)
```

```python
import functools
import math

import jax
import jax.numpy as jnp
from jax import lax
from jax.experimental import pallas as pl
from jax.experimental.pallas import tpu as pltpu
from jax.sharding import PartitionSpec as P

ITERS = 8
LANES = 128
PAIR = 2
CHUNK = 8
entropic = 0.1
relaxed = 1.0 / 1.1
MESH = pl.DeviceIdType.MESH


def split(x, pieces):
    out = []
    for k in range(pieces):
        out.append(x.astype(jnp.bfloat16).astype(jnp.float32))
        x = x - out[-1]
    return out


def peak_total(x):
    peak = jnp.max(x, axis=0)
    return peak, jnp.sum(jnp.exp2(x - peak[None]), axis=0)


def kernel(
    sizes, src_ref, smass_ref, tgt_ref, tmass_ref, fate_ref,
    f_ref, g_ref, out_ref,
    tt, ft, scores, log_b, g_scaled, log_a, f_scaled, row_peak, row_total, parts, f_parts,
    lhs, src_level, src_rows,
    tt_send, tt_recv, fwd_send, fwd_recv, ft_send, ft_recv, ex_send, ex_recv, f_send, f_recv,
):
    X, C, R, src_count, tgt_count, dim, fates = sizes
    rows = src_count // (R * PAIR)
    own = src_count // (C * R)
    blocks = C * R * tgt_count // LANES
    chunks = blocks // CHUNK
    per = tgt_count // LANES
    groups = rows // 8
    peers = X * PAIR * R
    x_id, c_id, r_id = lax.axis_index("rows"), lax.axis_index("cols"), lax.axis_index("rep")
    c_base = c_id // PAIR * PAIR
    shares = PAIR * R
    share = (c_id - c_base) * R + r_id
    me = x_id * shares + share
    all_sources, all_targets = src_count * X, tgt_count * C * R
    unit = math.log2(math.e) / (dim * entropic)

    def peer(step):
        other = lax.rem(me + step, peers)
        return {
            "rows": other // shares,
            "cols": c_base + lax.rem(other, shares) // R,
            "rep": lax.rem(other, R),
        }

    def share_of(step):
        other = lax.rem(share + step, shares)
        return {"cols": c_base + other // R, "rep": lax.rem(other, R)}

    def col_of(step):
        return lax.rem(c_id + step, C)

    def rep_of(step):
        return lax.rem(r_id + step, R)

    barrier = pltpu.get_barrier_semaphore()
    for step in range(1, peers):
        pl.semaphore_signal(barrier, inc=1, device_id=peer(step), device_id_type=MESH)
    for step in range(C):
        for turn in range(R):
            if step or turn:
                pl.semaphore_signal(
                    barrier, inc=1, device_id={"cols": col_of(step), "rep": rep_of(turn)},
                    device_id_type=MESH,
                )

    tt[c_id, r_id, 0:dim, :] = tgt_ref[...]
    ft[c_id, r_id, :, :] = fate_ref[...]
    tt[c_id, r_id, dim:dim + 8, :] = jnp.broadcast_to(
        jnp.log2(tmass_ref[...] / all_targets), (8, tgt_count)
    )

    for k in range(src_count // LANES):
        at = slice(k * LANES, (k + 1) * LANES)
        src_rows[at, :] = src_ref[:, at].T
    first = pl.multiple_of(share * rows, rows)
    first_own = pl.multiple_of((c_id * R + r_id) * own, own)
    mine = jnp.concatenate(
        [src_rows[pl.ds(first, rows), :], src_rows[pl.ds(first_own, own), :]], axis=0
    )
    src_level[...] = jnp.broadcast_to(
        jnp.sum(mine * mine, axis=1, keepdims=True) * unit, src_level.shape
    )
    a, b, c = split(mine * (2.0 * unit), 3)
    lhs[...] = jnp.concatenate([a, a, b, a, c, b], axis=1).astype(jnp.bfloat16)

    pl.semaphore_wait(barrier, peers - 1 + C * R - 1)

    def tt_copy(step):
        return pltpu.make_async_remote_copy(
            src_ref=tt.at[c_id, r_id], dst_ref=tt.at[c_id, r_id],
            send_sem=tt_send.at[step], recv_sem=tt_recv.at[c_id],
            device_id={"cols": col_of(step)}, device_id_type=MESH,
        )

    def fwd_copy(col, turn):
        return pltpu.make_async_remote_copy(
            src_ref=tt.at[col, r_id], dst_ref=tt.at[col, r_id],
            send_sem=fwd_send.at[col, turn], recv_sem=fwd_recv.at[col, r_id],
            device_id={"rep": rep_of(turn)}, device_id_type=MESH,
        )

    def ft_copy(step, turn):
        return pltpu.make_async_remote_copy(
            src_ref=ft.at[c_id, r_id], dst_ref=ft.at[c_id, r_id],
            send_sem=ft_send.at[step, turn], recv_sem=ft_recv.at[c_id, r_id],
            device_id={"cols": col_of(step), "rep": rep_of(turn)}, device_id_type=MESH,
        )

    def tt_arrived(col):
        pltpu.make_async_remote_copy(
            src_ref=tt.at[col, r_id], dst_ref=tt.at[col, r_id],
            send_sem=tt_send.at[0], recv_sem=tt_recv.at[col],
            device_id={"cols": col}, device_id_type=MESH,
        ).wait_recv()

    def fwd_arrived(col, rep):
        pltpu.make_async_remote_copy(
            src_ref=tt.at[col, rep], dst_ref=tt.at[col, rep],
            send_sem=fwd_send.at[col, 0], recv_sem=fwd_recv.at[col, rep],
            device_id={"rep": rep}, device_id_type=MESH,
        ).wait_recv()

    def ft_arrived(col, rep):
        pltpu.make_async_remote_copy(
            src_ref=ft.at[col, rep], dst_ref=ft.at[col, rep],
            send_sem=ft_send.at[0, 0], recv_sem=ft_recv.at[col, rep],
            device_id={"cols": col, "rep": rep}, device_id_type=MESH,
        ).wait_recv()

    for step in range(1, C):
        tt_copy(step).start()
    for turn in range(1, R):
        fwd_copy(c_id, turn).start()
    for step in list(range(1, C)) + [0]:
        for turn in range(R):
            if step or turn:
                ft_copy(step, turn).start()

    def fill(col, rep):
        block = tt[col, rep, 0:dim, :]
        a, b, c = [p.astype(jnp.bfloat16) for p in split(block, 3)]
        rhs = jnp.concatenate([a, b, a, c, a, b], axis=0)
        products = jnp.dot(lhs[...], rhs, preferred_element_type=jnp.float32)
        tgt_level = jnp.sum(block * block, axis=0, keepdims=True) * unit
        for k in range(per):
            at = (col * R + rep) * per + k
            lanes = slice(k * LANES, (k + 1) * LANES)
            scores[at] = products[:, lanes] - (src_level[...] + tgt_level[:, lanes])
            level = tt[col, rep, dim:dim + 8, k * LANES:(k + 1) * LANES]
            log_b[at] = level
            g_scaled[at] = level

    fill(c_id, r_id)
    for k in range(rows // LANES):
        level = jnp.log2(smass_ref[share, k:k + 1, :] / all_sources)
        log_a[k * LANES:(k + 1) * LANES, :] = jnp.broadcast_to(level, (LANES, LANES)).T
    for turn in range(1, R):
        fwd_arrived(c_id, rep_of(turn))
        fill(c_id, rep_of(turn))
    for step in range(1, C):
        tt_arrived(col_of(step))
        for turn in range(1, R):
            fwd_copy(col_of(step), turn).start()
        fill(col_of(step), r_id)
    for step in range(1, C):
        for turn in range(1, R):
            fwd_arrived(col_of(step), rep_of(turn))
            fill(col_of(step), rep_of(turn))

    def row_chunk(chunk):
        def row_group(group, carry):
            at = pl.multiple_of(group * 8, 8)
            base = chunk * CHUNK
            x = scores[pl.ds(base, CHUNK), pl.ds(at, 8), :] + g_scaled[pl.ds(base, CHUNK)]
            peak, total = peak_total(x)
            row_peak[chunk, pl.ds(at, 8), :] = peak
            row_total[chunk, pl.ds(at, 8), :] = total
            return carry

        lax.fori_loop(0, groups, row_group, 0, unroll=8)

    def row_finish():
        peaks = row_peak[...]
        top = jnp.max(jnp.max(peaks, axis=0), axis=1, keepdims=True)
        totals = jnp.sum(row_total[...] * jnp.exp2(peaks - top[None]), axis=0)
        level = top + jnp.log2(jnp.sum(totals, axis=1, keepdims=True))
        f_scaled[...] = log_a[...] - relaxed * level

    def col_block(block):
        peaks, totals = [], []
        for q in range(rows // LANES):
            at = slice(q * LANES, (q + 1) * LANES)
            x = (scores[block, at, :] + f_scaled[at, :]).reshape(LANES // 8, 8, LANES)
            peak, total = peak_total(x)
            peaks.append(peak)
            totals.append(total)
        top = jnp.max(functools.reduce(jnp.maximum, peaks), axis=0, keepdims=True)
        whole = sum(t * jnp.exp2(p - top) for p, t in zip(peaks, totals))
        return top + jnp.log2(jnp.sum(whole, axis=0, keepdims=True))

    def ex_copy(slot, chunk, step):
        return pltpu.make_async_remote_copy(
            src_ref=parts.at[slot, chunk, me], dst_ref=parts.at[slot, chunk, me],
            send_sem=ex_send.at[slot, chunk, step], recv_sem=ex_recv.at[slot, chunk, me],
            device_id=peer(step), device_id_type=MESH,
        )

    def ex_arrived(slot, chunk, step):
        other = lax.rem(me + step, peers)
        pltpu.make_async_remote_copy(
            src_ref=parts.at[slot, chunk, other], dst_ref=parts.at[slot, chunk, other],
            send_sem=ex_send.at[slot, chunk, 0], recv_sem=ex_recv.at[slot, chunk, other],
            device_id=peer(step), device_id_type=MESH,
        ).wait_recv()

    for chunk in range(chunks):
        row_chunk(chunk)

    def iteration(it, carry):
        slot = lax.rem(it, 2)
        row_finish()
        for chunk in range(chunks):
            for j in range(CHUNK):
                parts[slot, chunk, me, j:j + 1, :] = col_block(chunk * CHUNK + j)
            for step in range(1, peers):
                ex_copy(slot, chunk, step).start()
        for chunk in range(chunks):
            for step in range(1, peers):
                ex_arrived(slot, chunk, step)
            peak, total = peak_total(parts[slot, chunk])
            level = -relaxed * (peak + jnp.log2(total))
            for j in range(CHUNK):
                g_scaled[chunk * CHUNK + j] = (
                    jnp.broadcast_to(level[j:j + 1, :], (8, LANES)) + log_b[chunk * CHUNK + j]
                )
            row_chunk(chunk)
        for chunk in range(chunks):
            for step in range(1, peers):
                ex_copy(slot, chunk, step).wait_send()
        return carry

    lax.fori_loop(0, ITERS, iteration, 0)

    back = entropic * math.log(2.0)
    for k in range(rows // LANES):
        at = slice(k * LANES, (k + 1) * LANES)
        turned = ((f_scaled[at, :] - log_a[at, :]) * back).T
        f_parts[share, k:k + 1, :] = turned[0:1, :]

    def f_copy(turn):
        return pltpu.make_async_remote_copy(
            src_ref=f_parts.at[share], dst_ref=f_parts.at[share],
            send_sem=f_send.at[turn], recv_sem=f_recv.at[share],
            device_id=share_of(turn), device_id_type=MESH,
        )

    for turn in range(1, shares):
        f_copy(turn).start()
    for k in range(per):
        at = (c_id * R + r_id) * per + k
        g_ref[k:k + 1, :] = ((g_scaled[at] - log_b[at]) * back)[0:1, :]

    def own_scores(block):
        return scores[block, rows:rows + own, :].reshape(own // 8, 8, LANES) + g_scaled[block][None]

    def own_peak(block, peak):
        return jnp.maximum(peak, own_scores(block))

    peak = lax.fori_loop(1, blocks, own_peak, own_scores(0), unroll=5)
    top = jnp.max(peak, axis=2, keepdims=True)
    for step in range(C):
        for turn in range(R):
            if step or turn:
                ft_arrived(col_of(step), rep_of(turn))

    def across(left, right):
        return lax.dot_general(
            left, right, (((1,), (1,)), ((), ())), preferred_element_type=jnp.float32
        )

    def fate_block(block, carry):
        total, weighted = carry
        pieces = [jnp.exp2(own_scores(block * per + k) - top) for k in range(per)]
        total = total + sum(pieces)
        weights = jnp.concatenate([p.reshape(own, LANES) for p in pieces], axis=1)
        high, low = [p.astype(jnp.bfloat16) for p in split(weights, 2)]
        panel = [p.astype(jnp.bfloat16) for p in split(ft[block // R, lax.rem(block, R)], 2)]
        return total, weighted + across(high, jnp.concatenate(panel, axis=0)) + across(
            low, jnp.concatenate([panel[0], jnp.zeros_like(panel[0])], axis=0)
        )

    total, weighted = lax.fori_loop(
        0, C * R, fate_block,
        (jnp.zeros((own // 8, 8, LANES), jnp.float32), jnp.zeros((own, 2 * fates), jnp.float32)),
    )
    weighted = weighted / jnp.sum(total.reshape(own, LANES), axis=1, keepdims=True)
    turned = weighted.T
    out_ref[...] = turned[:fates] + turned[fates:]
    for turn in range(1, shares):
        other = lax.rem(share + turn, shares)
        pltpu.make_async_remote_copy(
            src_ref=f_parts.at[other], dst_ref=f_parts.at[other],
            send_sem=f_send.at[0], recv_sem=f_recv.at[other],
            device_id=share_of(turn), device_id_type=MESH,
        ).wait_recv()
    f_ref[...] = f_parts[...]

    for turn in range(1, shares):
        f_copy(turn).wait_send()
    for turn in range(1, R):
        for step in range(C):
            fwd_copy(col_of(step), turn).wait_send()
    for step in range(1, C):
        tt_copy(step).wait_send()
    for step in range(C):
        for turn in range(R):
            if step or turn:
                ft_copy(step, turn).wait_send()


def solution(mesh):
    X, C, R = mesh.shape["rows"], mesh.shape["cols"], mesh.shape["rep"]

    def body(sources, source_mass, targets, target_mass, fate_panel):
        src_count, dim = sources.shape
        tgt_count, fates = fate_panel.shape
        shares = PAIR * R
        rows, own = src_count // shares, src_count // (C * R)
        blocks = C * R * tgt_count // LANES
        chunks = blocks // CHUNK
        peers = X * shares
        vmem = pl.BlockSpec(memory_space=pltpu.VMEM)
        dma = pltpu.SemaphoreType.DMA
        f32 = jnp.float32
        f_pot, g_pot, fate_rows = pl.pallas_call(
            functools.partial(kernel, (X, C, R, src_count, tgt_count, dim, fates)),
            out_shape=(
                jax.ShapeDtypeStruct((shares, rows // LANES, LANES), f32),
                jax.ShapeDtypeStruct((tgt_count // LANES, LANES), f32),
                jax.ShapeDtypeStruct((fates, own), f32),
            ),
            in_specs=[vmem] * 5,
            out_specs=(vmem,) * 3,
            scratch_shapes=[
                pltpu.VMEM((C, R, dim + 8, tgt_count), f32),
                pltpu.VMEM((C, R, fates, tgt_count), f32),
                pltpu.VMEM((blocks, rows + own, LANES), f32),
                pltpu.VMEM((blocks, 8, LANES), f32),
                pltpu.VMEM((blocks, 8, LANES), f32),
                pltpu.VMEM((rows, LANES), f32),
                pltpu.VMEM((rows, LANES), f32),
                pltpu.VMEM((chunks, rows, LANES), f32),
                pltpu.VMEM((chunks, rows, LANES), f32),
                pltpu.VMEM((2, chunks, peers, CHUNK, LANES), f32),
                pltpu.VMEM((shares, rows // LANES, LANES), f32),
                pltpu.VMEM((rows + own, 6 * dim), jnp.bfloat16),
                pltpu.VMEM((rows + own, LANES), f32),
                pltpu.VMEM((src_count, dim), f32),
                dma((C,)), dma((C,)),
                dma((C, R)), dma((C, R)),
                dma((C, R)), dma((C, R)),
                dma((2, chunks, peers)), dma((2, chunks, peers)),
                dma((shares,)), dma((shares,)),
            ],
            compiler_params=pltpu.CompilerParams(
                collective_id=0, has_side_effects=True, vmem_limit_bytes=48 * 2**20
            ),
            name="transport",
        )(
            sources.T,
            source_mass.reshape(shares, rows // LANES, LANES),
            targets.T,
            target_mass.reshape(1, tgt_count),
            fate_panel.T,
        )
        return f_pot.reshape(src_count), g_pot.reshape(tgt_count), fate_rows.T

    in_specs = (
        P(("parts", "rows"), None),
        P(("parts", "rows")),
        P(("parts", "cols", "rep"), None),
        P(("parts", "cols", "rep")),
        P(("parts", "cols", "rep"), None),
    )
    out_specs = (
        P(("parts", "rows")),
        P(("parts", "cols", "rep")),
        P(("parts", "rows", "cols", "rep"), None),
    )
    return jax.shard_map(body, mesh=mesh, in_specs=in_specs, out_specs=out_specs, check_vma=False)
```

```python
import functools
import math

import jax
import jax.numpy as jnp
from jax import lax
from jax.experimental import pallas as pl
from jax.experimental.pallas import tpu as pltpu
from jax.sharding import PartitionSpec as P

ITERS = 8
LANES = 128
PAIR = 1
CHUNK = 8
entropic = 0.1
relaxed = 1.0 / 1.1
MESH = pl.DeviceIdType.MESH


def split(x, pieces):
    out = []
    for k in range(pieces):
        out.append(x.astype(jnp.bfloat16).astype(jnp.float32))
        x = x - out[-1]
    return out


def peak_total(x):
    peak = jnp.max(x, axis=0)
    return peak, jnp.sum(jnp.exp2(x - peak[None]), axis=0)


def kernel(
    sizes, src_ref, smass_ref, tgt_ref, tmass_ref, fate_ref,
    f_ref, g_ref, out_ref,
    tt, ft, scores, log_b, g_scaled, log_a, f_scaled, row_peak, row_total, parts, f_parts,
    lhs, src_level, src_rows,
    tt_send, tt_recv, fwd_send, fwd_recv, ft_send, ft_recv, ex_send, ex_recv, f_send, f_recv,
):
    X, C, R, src_count, tgt_count, dim, fates = sizes
    rows = src_count // (R * PAIR)
    own = src_count // (C * R)
    blocks = C * R * tgt_count // LANES
    chunks = blocks // CHUNK
    per = tgt_count // LANES
    width = CHUNK // (R * per)
    groups = rows // 8
    peers = X * PAIR * R
    x_id, c_id, r_id = lax.axis_index("rows"), lax.axis_index("cols"), lax.axis_index("rep")
    c_base = c_id // PAIR * PAIR
    shares = PAIR * R
    share = (c_id - c_base) * R + r_id
    me = x_id * shares + share
    all_sources, all_targets = src_count * X, tgt_count * C * R
    unit = math.log2(math.e) / (dim * entropic)

    def peer(step):
        other = lax.rem(me + step, peers)
        return {
            "rows": other // shares,
            "cols": c_base + lax.rem(other, shares) // R,
            "rep": lax.rem(other, R),
        }

    def share_of(step):
        other = lax.rem(share + step, shares)
        return {"cols": c_base + other // R, "rep": lax.rem(other, R)}

    def col_of(step):
        return lax.rem(c_id + step, C)

    def rep_of(step):
        return lax.rem(r_id + step, R)

    barrier = pltpu.get_barrier_semaphore()
    for step in range(1, peers):
        pl.semaphore_signal(barrier, inc=1, device_id=peer(step), device_id_type=MESH)
    for step in range(C):
        for turn in range(R):
            if step or turn:
                pl.semaphore_signal(
                    barrier, inc=1, device_id={"cols": col_of(step), "rep": rep_of(turn)},
                    device_id_type=MESH,
                )

    tt[c_id, r_id, 0:dim, :] = tgt_ref[...]
    ft[c_id, r_id, :, :] = fate_ref[...]
    tt[c_id, r_id, dim:dim + 8, :] = jnp.broadcast_to(
        jnp.log2(tmass_ref[...] / all_targets), (8, tgt_count)
    )

    for k in range(src_count // LANES):
        at = slice(k * LANES, (k + 1) * LANES)
        src_rows[at, :] = src_ref[:, at].T
    first = pl.multiple_of(share * rows, rows)
    first_own = pl.multiple_of((c_id * R + r_id) * own, own)
    mine = jnp.concatenate(
        [src_rows[pl.ds(first, rows), :], src_rows[pl.ds(first_own, own), :]], axis=0
    )
    src_level[...] = jnp.broadcast_to(
        jnp.sum(mine * mine, axis=1, keepdims=True) * unit, src_level.shape
    )
    a, b, c = split(mine * (2.0 * unit), 3)
    lhs[...] = jnp.concatenate([a, a, b, a, c, b], axis=1).astype(jnp.bfloat16)

    pl.semaphore_wait(barrier, peers - 1 + C * R - 1)

    def tt_copy(step):
        return pltpu.make_async_remote_copy(
            src_ref=tt.at[c_id, r_id], dst_ref=tt.at[c_id, r_id],
            send_sem=tt_send.at[step], recv_sem=tt_recv.at[c_id],
            device_id={"cols": col_of(step)}, device_id_type=MESH,
        )

    def fwd_copy(col, turn):
        return pltpu.make_async_remote_copy(
            src_ref=tt.at[col, r_id], dst_ref=tt.at[col, r_id],
            send_sem=fwd_send.at[col, turn], recv_sem=fwd_recv.at[col, r_id],
            device_id={"rep": rep_of(turn)}, device_id_type=MESH,
        )

    def ft_copy(step, turn):
        return pltpu.make_async_remote_copy(
            src_ref=ft.at[c_id, r_id], dst_ref=ft.at[c_id, r_id],
            send_sem=ft_send.at[step, turn], recv_sem=ft_recv.at[c_id, r_id],
            device_id={"cols": col_of(step), "rep": rep_of(turn)}, device_id_type=MESH,
        )

    def tt_arrived(col):
        pltpu.make_async_remote_copy(
            src_ref=tt.at[col, r_id], dst_ref=tt.at[col, r_id],
            send_sem=tt_send.at[0], recv_sem=tt_recv.at[col],
            device_id={"cols": col}, device_id_type=MESH,
        ).wait_recv()

    def fwd_arrived(col, rep):
        pltpu.make_async_remote_copy(
            src_ref=tt.at[col, rep], dst_ref=tt.at[col, rep],
            send_sem=fwd_send.at[col, 0], recv_sem=fwd_recv.at[col, rep],
            device_id={"rep": rep}, device_id_type=MESH,
        ).wait_recv()

    def ft_arrived(col, rep):
        pltpu.make_async_remote_copy(
            src_ref=ft.at[col, rep], dst_ref=ft.at[col, rep],
            send_sem=ft_send.at[0, 0], recv_sem=ft_recv.at[col, rep],
            device_id={"cols": col, "rep": rep}, device_id_type=MESH,
        ).wait_recv()

    for step in range(1, C):
        tt_copy(step).start()
    for turn in range(1, R):
        fwd_copy(c_id, turn).start()
    for step in list(range(1, C)) + [0]:
        for turn in range(R):
            if step or turn:
                ft_copy(step, turn).start()

    def fill(col, rep):
        block = tt[col, rep, 0:dim, :]
        a, b, c = [p.astype(jnp.bfloat16) for p in split(block, 3)]
        rhs = jnp.concatenate([a, b, a, c, a, b], axis=0)
        products = jnp.dot(lhs[...], rhs, preferred_element_type=jnp.float32)
        tgt_level = jnp.sum(block * block, axis=0, keepdims=True) * unit
        for k in range(per):
            at = (col * R + rep) * per + k
            lanes = slice(k * LANES, (k + 1) * LANES)
            scores[at] = products[:, lanes] - (src_level[...] + tgt_level[:, lanes])
            level = tt[col, rep, dim:dim + 8, k * LANES:(k + 1) * LANES]
            log_b[at] = level
            g_scaled[at] = level

    def row_chunk(chunk):
        base = chunk * CHUNK
        g_chunk = g_scaled[pl.ds(base, CHUNK)]

        def row_group(group, carry):
            at = pl.multiple_of(group * 8, 8)
            x = scores[pl.ds(base, CHUNK), pl.ds(at, 8), :] + g_chunk
            peak, total = peak_total(x)
            row_peak[chunk, pl.ds(at, 8), :] = peak
            row_total[chunk, pl.ds(at, 8), :] = total
            return carry

        lax.fori_loop(0, groups, row_group, 0, unroll=8)

    def row_finish():
        peaks = row_peak[...]
        top = jnp.max(jnp.max(peaks, axis=0), axis=1, keepdims=True)
        totals = jnp.sum(row_total[...] * jnp.exp2(peaks - top[None]), axis=0)
        level = top + jnp.log2(jnp.sum(totals, axis=1, keepdims=True))
        f_scaled[...] = log_a[...] - relaxed * level

    def col_blocks(blocks):
        peaks, totals = [[] for b in blocks], [[] for b in blocks]
        for q in range(rows // LANES):
            at = slice(q * LANES, (q + 1) * LANES)
            f_rows = f_scaled[at, :]
            for k, block in enumerate(blocks):
                x = (scores[block, at, :] + f_rows).reshape(LANES // 8, 8, LANES)
                peak, total = peak_total(x)
                peaks[k].append(peak)
                totals[k].append(total)
        for k in range(len(blocks)):
            top = jnp.max(functools.reduce(jnp.maximum, peaks[k]), axis=0, keepdims=True)
            whole = sum(t * jnp.exp2(p - top) for p, t in zip(peaks[k], totals[k]))
            yield top + jnp.log2(jnp.sum(whole, axis=0, keepdims=True))

    def ex_copy(slot, chunk, step):
        return pltpu.make_async_remote_copy(
            src_ref=parts.at[slot, chunk, me], dst_ref=parts.at[slot, chunk, me],
            send_sem=ex_send.at[slot, chunk, step], recv_sem=ex_recv.at[slot, chunk, me],
            device_id=peer(step), device_id_type=MESH,
        )

    def ex_arrived(slot, chunk, step):
        other = lax.rem(me + step, peers)
        pltpu.make_async_remote_copy(
            src_ref=parts.at[slot, chunk, other], dst_ref=parts.at[slot, chunk, other],
            send_sem=ex_send.at[slot, chunk, 0], recv_sem=ex_recv.at[slot, chunk, other],
            device_id=peer(step), device_id_type=MESH,
        ).wait_recv()

    fill(c_id, r_id)
    for k in range(rows // LANES):
        level = jnp.log2(smass_ref[share, k:k + 1, :] / all_sources)
        log_a[k * LANES:(k + 1) * LANES, :] = jnp.broadcast_to(level, (LANES, LANES)).T
    for turn in range(1, R):
        fwd_arrived(c_id, rep_of(turn))
        fill(c_id, rep_of(turn))
    ready = None
    for p in range(chunks):
        chunk = lax.rem(c_id // width + p, chunks)
        if p:
            cols = [chunk * width + k for k in range(width)]
        else:
            cols = [chunk * width + lax.rem(c_id + k, width) for k in range(1, width)]
        for col in cols:
            tt_arrived(col)
            for turn in range(1, R):
                fwd_copy(col, turn).start()
            fill(col, r_id)
        if ready is not None:
            row_chunk(ready)
        for col in cols:
            for turn in range(1, R):
                fwd_arrived(col, rep_of(turn))
                fill(col, rep_of(turn))
        ready = chunk
    row_chunk(ready)

    def iteration(it, carry):
        slot = lax.rem(it, 2)
        row_finish()
        for chunk in range(chunks):
            levels = []
            for j in range(0, CHUNK, 2):
                levels += col_blocks([chunk * CHUNK + j, chunk * CHUNK + j + 1])
            parts[slot, chunk, me] = jnp.concatenate(levels, axis=0)
            for step in range(1, peers):
                ex_copy(slot, chunk, step).start()
        for chunk in range(chunks):
            for step in range(1, peers):
                ex_arrived(slot, chunk, step)
            peak, total = peak_total(parts[slot, chunk])
            level = -relaxed * (peak + jnp.log2(total))
            for j in range(CHUNK):
                g_scaled[chunk * CHUNK + j] = (
                    jnp.broadcast_to(level[j:j + 1, :], (8, LANES)) + log_b[chunk * CHUNK + j]
                )
            row_chunk(chunk)
        for chunk in range(chunks):
            for step in range(1, peers):
                ex_copy(slot, chunk, step).wait_send()
        return carry

    lax.fori_loop(0, ITERS, iteration, 0)

    back = entropic * math.log(2.0)
    for k in range(rows // LANES):
        at = slice(k * LANES, (k + 1) * LANES)
        turned = ((f_scaled[at, :] - log_a[at, :]) * back).T
        f_parts[share, k:k + 1, :] = turned[0:1, :]

    def f_copy(turn):
        return pltpu.make_async_remote_copy(
            src_ref=f_parts.at[share], dst_ref=f_parts.at[share],
            send_sem=f_send.at[turn], recv_sem=f_recv.at[share],
            device_id=share_of(turn), device_id_type=MESH,
        )

    for turn in range(1, shares):
        f_copy(turn).start()
    for k in range(per):
        at = (c_id * R + r_id) * per + k
        g_ref[k:k + 1, :] = ((g_scaled[at] - log_b[at]) * back)[0:1, :]

    def own_scores(block):
        return scores[block, rows:rows + own, :].reshape(own // 8, 8, LANES) + g_scaled[block][None]

    def own_peak(block, peak):
        return jnp.maximum(peak, own_scores(block))

    peak = lax.fori_loop(1, blocks, own_peak, own_scores(0), unroll=5)
    top = jnp.max(peak, axis=2, keepdims=True)
    for step in range(C):
        for turn in range(R):
            if step or turn:
                ft_arrived(col_of(step), rep_of(turn))

    def across(left, right):
        return lax.dot_general(
            left, right, (((1,), (1,)), ((), ())), preferred_element_type=jnp.float32
        )

    def fate_block(block, carry):
        total, weighted = carry
        pieces = [jnp.exp2(own_scores(block * per + k) - top) for k in range(per)]
        total = total + sum(pieces)
        weights = jnp.concatenate([p.reshape(own, LANES) for p in pieces], axis=1)
        high, low = [p.astype(jnp.bfloat16) for p in split(weights, 2)]
        panel = [p.astype(jnp.bfloat16) for p in split(ft[block // R, lax.rem(block, R)], 2)]
        return total, weighted + across(high, jnp.concatenate(panel, axis=0)) + across(
            low, jnp.concatenate([panel[0], jnp.zeros_like(panel[0])], axis=0)
        )

    total, weighted = lax.fori_loop(
        0, C * R, fate_block,
        (jnp.zeros((own // 8, 8, LANES), jnp.float32), jnp.zeros((own, 2 * fates), jnp.float32)),
    )
    weighted = weighted / jnp.sum(total.reshape(own, LANES), axis=1, keepdims=True)
    turned = weighted.T
    out_ref[...] = turned[:fates] + turned[fates:]
    for turn in range(1, shares):
        other = lax.rem(share + turn, shares)
        pltpu.make_async_remote_copy(
            src_ref=f_parts.at[other], dst_ref=f_parts.at[other],
            send_sem=f_send.at[0], recv_sem=f_recv.at[other],
            device_id=share_of(turn), device_id_type=MESH,
        ).wait_recv()
    f_ref[...] = f_parts[...]

    for turn in range(1, shares):
        f_copy(turn).wait_send()
    for turn in range(1, R):
        for step in range(C):
            fwd_copy(col_of(step), turn).wait_send()
    for step in range(1, C):
        tt_copy(step).wait_send()
    for step in range(C):
        for turn in range(R):
            if step or turn:
                ft_copy(step, turn).wait_send()


def solution(mesh):
    X, C, R = mesh.shape["rows"], mesh.shape["cols"], mesh.shape["rep"]

    def body(sources, source_mass, targets, target_mass, fate_panel):
        src_count, dim = sources.shape
        tgt_count, fates = fate_panel.shape
        shares = PAIR * R
        rows, own = src_count // shares, src_count // (C * R)
        blocks = C * R * tgt_count // LANES
        chunks = blocks // CHUNK
        peers = X * shares
        vmem = pl.BlockSpec(memory_space=pltpu.VMEM)
        dma = pltpu.SemaphoreType.DMA
        f32 = jnp.float32
        f_pot, g_pot, fate_rows = pl.pallas_call(
            functools.partial(kernel, (X, C, R, src_count, tgt_count, dim, fates)),
            out_shape=(
                jax.ShapeDtypeStruct((shares, rows // LANES, LANES), f32),
                jax.ShapeDtypeStruct((tgt_count // LANES, LANES), f32),
                jax.ShapeDtypeStruct((fates, own), f32),
            ),
            in_specs=[vmem] * 5,
            out_specs=(vmem,) * 3,
            scratch_shapes=[
                pltpu.VMEM((C, R, dim + 8, tgt_count), f32),
                pltpu.VMEM((C, R, fates, tgt_count), f32),
                pltpu.VMEM((blocks, rows + own, LANES), f32),
                pltpu.VMEM((blocks, 8, LANES), f32),
                pltpu.VMEM((blocks, 8, LANES), f32),
                pltpu.VMEM((rows, LANES), f32),
                pltpu.VMEM((rows, LANES), f32),
                pltpu.VMEM((chunks, rows, LANES), f32),
                pltpu.VMEM((chunks, rows, LANES), f32),
                pltpu.VMEM((2, chunks, peers, CHUNK, LANES), f32),
                pltpu.VMEM((shares, rows // LANES, LANES), f32),
                pltpu.VMEM((rows + own, 6 * dim), jnp.bfloat16),
                pltpu.VMEM((rows + own, LANES), f32),
                pltpu.VMEM((src_count, dim), f32),
                dma((C,)), dma((C,)),
                dma((C, R)), dma((C, R)),
                dma((C, R)), dma((C, R)),
                dma((2, chunks, peers)), dma((2, chunks, peers)),
                dma((shares,)), dma((shares,)),
            ],
            compiler_params=pltpu.CompilerParams(
                collective_id=0, has_side_effects=True, vmem_limit_bytes=48 * 2**20
            ),
            name="transport",
        )(
            sources.T,
            source_mass.reshape(shares, rows // LANES, LANES),
            targets.T,
            target_mass.reshape(1, tgt_count),
            fate_panel.T,
        )
        return f_pot.reshape(src_count), g_pot.reshape(tgt_count), fate_rows.T

    in_specs = (
        P(("parts", "rows"), None),
        P(("parts", "rows")),
        P(("parts", "cols", "rep"), None),
        P(("parts", "cols", "rep")),
        P(("parts", "cols", "rep"), None),
    )
    out_specs = (
        P(("parts", "rows")),
        P(("parts", "cols", "rep")),
        P(("parts", "rows", "cols", "rep"), None),
    )
    return jax.shard_map(body, mesh=mesh, in_specs=in_specs, out_specs=out_specs, check_vma=False)
```

```python
import functools
import math

import jax
import jax.numpy as jnp
from jax import lax
from jax.experimental import pallas as pl
from jax.experimental.pallas import tpu as pltpu
from jax.sharding import PartitionSpec as P

ITERS = 8
LANES = 128
PAIR = 1
CHUNK = 8
entropic = 0.1
relaxed = 1.0 / 1.1
MESH = pl.DeviceIdType.MESH


def split(x, pieces):
    out = []
    for k in range(pieces):
        out.append(x.astype(jnp.bfloat16).astype(jnp.float32))
        x = x - out[-1]
    return out


def peak_total(x):
    peak = jnp.max(x, axis=0)
    return peak, jnp.sum(jnp.exp2(x - peak[None]), axis=0)


def kernel(
    sizes, src_ref, smass_ref, tgt_ref, tmass_ref, fate_ref,
    f_ref, g_ref, out_ref,
    tt, ft, scores, log_b, g_scaled, log_a, f_scaled, row_peak, row_total, parts, f_parts,
    lhs, src_level, src_rows,
    tt_send, tt_recv, fwd_send, fwd_recv, ft_send, ft_recv, ex_send, ex_recv, f_send, f_recv,
):
    X, C, R, src_count, tgt_count, dim, fates = sizes
    rows = src_count // (R * PAIR)
    own = src_count // (C * R)
    blocks = C * R * tgt_count // LANES
    chunks = blocks // CHUNK
    per = tgt_count // LANES
    width = CHUNK // (R * per)
    groups = rows // 8
    peers = X * PAIR * R
    x_id, c_id, r_id = lax.axis_index("rows"), lax.axis_index("cols"), lax.axis_index("rep")
    c_base = c_id // PAIR * PAIR
    shares = PAIR * R
    share = (c_id - c_base) * R + r_id
    me = x_id * shares + share
    all_sources, all_targets = src_count * X, tgt_count * C * R
    unit = math.log2(math.e) / (dim * entropic)

    def peer(step):
        other = lax.rem(me + step, peers)
        return {
            "rows": other // shares,
            "cols": c_base + lax.rem(other, shares) // R,
            "rep": lax.rem(other, R),
        }

    def share_of(step):
        other = lax.rem(share + step, shares)
        return {"cols": c_base + other // R, "rep": lax.rem(other, R)}

    def col_of(step):
        return lax.rem(c_id + step, C)

    def rep_of(step):
        return lax.rem(r_id + step, R)

    barrier = pltpu.get_barrier_semaphore()
    for step in range(1, peers):
        pl.semaphore_signal(barrier, inc=1, device_id=peer(step), device_id_type=MESH)
    for step in range(C):
        for turn in range(R):
            if step or turn:
                pl.semaphore_signal(
                    barrier, inc=1, device_id={"cols": col_of(step), "rep": rep_of(turn)},
                    device_id_type=MESH,
                )

    tt[c_id, r_id, 0:dim, :] = tgt_ref[...]
    ft[c_id, r_id, :, :] = fate_ref[...]
    tt[c_id, r_id, dim:dim + 8, :] = jnp.broadcast_to(
        jnp.log2(tmass_ref[...] / all_targets), (8, tgt_count)
    )

    pl.semaphore_wait(barrier, peers - 1 + C * R - 1)

    def tt_copy(step):
        return pltpu.make_async_remote_copy(
            src_ref=tt.at[c_id, r_id], dst_ref=tt.at[c_id, r_id],
            send_sem=tt_send.at[step], recv_sem=tt_recv.at[c_id],
            device_id={"cols": col_of(step)}, device_id_type=MESH,
        )

    def fwd_copy(col, turn):
        return pltpu.make_async_remote_copy(
            src_ref=tt.at[col, r_id], dst_ref=tt.at[col, r_id],
            send_sem=fwd_send.at[col, turn], recv_sem=fwd_recv.at[col, r_id],
            device_id={"rep": rep_of(turn)}, device_id_type=MESH,
        )

    def ft_copy(step, turn):
        return pltpu.make_async_remote_copy(
            src_ref=ft.at[c_id, r_id], dst_ref=ft.at[c_id, r_id],
            send_sem=ft_send.at[step, turn], recv_sem=ft_recv.at[c_id, r_id],
            device_id={"cols": col_of(step), "rep": rep_of(turn)}, device_id_type=MESH,
        )

    def tt_arrived(col):
        pltpu.make_async_remote_copy(
            src_ref=tt.at[col, r_id], dst_ref=tt.at[col, r_id],
            send_sem=tt_send.at[0], recv_sem=tt_recv.at[col],
            device_id={"cols": col}, device_id_type=MESH,
        ).wait_recv()

    def fwd_arrived(col, rep):
        pltpu.make_async_remote_copy(
            src_ref=tt.at[col, rep], dst_ref=tt.at[col, rep],
            send_sem=fwd_send.at[col, 0], recv_sem=fwd_recv.at[col, rep],
            device_id={"rep": rep}, device_id_type=MESH,
        ).wait_recv()

    def ft_arrived(col, rep):
        pltpu.make_async_remote_copy(
            src_ref=ft.at[col, rep], dst_ref=ft.at[col, rep],
            send_sem=ft_send.at[0, 0], recv_sem=ft_recv.at[col, rep],
            device_id={"cols": col, "rep": rep}, device_id_type=MESH,
        ).wait_recv()

    for step in range(1, C):
        tt_copy(step).start()
    for turn in range(1, R):
        fwd_copy(c_id, turn).start()
    for k in range(src_count // LANES):
        at = slice(k * LANES, (k + 1) * LANES)
        src_rows[at, :] = src_ref[:, at].T
    first = pl.multiple_of(share * rows, rows)
    first_own = pl.multiple_of((c_id * R + r_id) * own, own)
    mine = jnp.concatenate(
        [src_rows[pl.ds(first, rows), :], src_rows[pl.ds(first_own, own), :]], axis=0
    )
    src_level[...] = jnp.broadcast_to(
        jnp.sum(mine * mine, axis=1, keepdims=True) * unit, src_level.shape
    )
    a, b, c = split(mine * (2.0 * unit), 3)
    lhs[...] = jnp.concatenate([a, a, b, a, c, b], axis=1).astype(jnp.bfloat16)


    def fill(col, rep):
        block = tt[col, rep, 0:dim, :]
        a, b, c = [p.astype(jnp.bfloat16) for p in split(block, 3)]
        rhs = jnp.concatenate([a, b, a, c, a, b], axis=0)
        products = jnp.dot(lhs[...], rhs, preferred_element_type=jnp.float32)
        tgt_level = jnp.sum(block * block, axis=0, keepdims=True) * unit
        for k in range(per):
            at = (col * R + rep) * per + k
            lanes = slice(k * LANES, (k + 1) * LANES)
            scores[at] = products[:, lanes] - (src_level[...] + tgt_level[:, lanes])
            level = tt[col, rep, dim:dim + 8, k * LANES:(k + 1) * LANES]
            log_b[at] = level
            g_scaled[at] = level

    def row_chunk(chunk):
        base = chunk * CHUNK
        g_chunk = g_scaled[pl.ds(base, CHUNK)]

        def row_group(group, carry):
            at = pl.multiple_of(group * 8, 8)
            x = scores[pl.ds(base, CHUNK), pl.ds(at, 8), :] + g_chunk
            peak, total = peak_total(x)
            row_peak[chunk, pl.ds(at, 8), :] = peak
            row_total[chunk, pl.ds(at, 8), :] = total
            return carry

        lax.fori_loop(0, groups, row_group, 0, unroll=8)

    def row_finish():
        peaks = row_peak[...]
        top = jnp.max(jnp.max(peaks, axis=0), axis=1, keepdims=True)
        totals = jnp.sum(row_total[...] * jnp.exp2(peaks - top[None]), axis=0)
        level = top + jnp.log2(jnp.sum(totals, axis=1, keepdims=True))
        f_scaled[...] = log_a[...] - relaxed * level

    def col_blocks(blocks):
        peaks, totals = [[] for b in blocks], [[] for b in blocks]
        for q in range(rows // LANES):
            at = slice(q * LANES, (q + 1) * LANES)
            f_rows = f_scaled[at, :]
            for k, block in enumerate(blocks):
                x = (scores[block, at, :] + f_rows).reshape(LANES // 8, 8, LANES)
                peak, total = peak_total(x)
                peaks[k].append(peak)
                totals[k].append(total)
        for k in range(len(blocks)):
            top = jnp.max(functools.reduce(jnp.maximum, peaks[k]), axis=0, keepdims=True)
            whole = sum(t * jnp.exp2(p - top) for p, t in zip(peaks[k], totals[k]))
            yield top + jnp.log2(jnp.sum(whole, axis=0, keepdims=True))

    def ex_copy(slot, chunk, step):
        return pltpu.make_async_remote_copy(
            src_ref=parts.at[slot, chunk, me], dst_ref=parts.at[slot, chunk, me],
            send_sem=ex_send.at[slot, chunk, step], recv_sem=ex_recv.at[slot, chunk, me],
            device_id=peer(step), device_id_type=MESH,
        )

    def ex_arrived(slot, chunk, step):
        other = lax.rem(me + step, peers)
        pltpu.make_async_remote_copy(
            src_ref=parts.at[slot, chunk, other], dst_ref=parts.at[slot, chunk, other],
            send_sem=ex_send.at[slot, chunk, 0], recv_sem=ex_recv.at[slot, chunk, other],
            device_id=peer(step), device_id_type=MESH,
        ).wait_recv()

    fill(c_id, r_id)
    for k in range(rows // LANES):
        level = jnp.log2(smass_ref[share, k:k + 1, :] / all_sources)
        log_a[k * LANES:(k + 1) * LANES, :] = jnp.broadcast_to(level, (LANES, LANES)).T
    for turn in range(1, R):
        fwd_arrived(c_id, rep_of(turn))
        fill(c_id, rep_of(turn))
    ready = None
    for p in range(chunks):
        chunk = lax.rem(c_id // width + p, chunks)
        if p:
            cols = [chunk * width + k for k in range(width)]
        else:
            cols = [chunk * width + lax.rem(c_id + k, width) for k in range(1, width)]
        for col in cols:
            tt_arrived(col)
            for turn in range(1, R):
                fwd_copy(col, turn).start()
            fill(col, r_id)
        if ready is not None:
            row_chunk(ready)
        for col in cols:
            for turn in range(1, R):
                fwd_arrived(col, rep_of(turn))
                fill(col, rep_of(turn))
        ready = chunk
    for step in list(range(1, C)) + [0]:
        for turn in range(R):
            if step or turn:
                ft_copy(step, turn).start()
    row_chunk(ready)

    def iteration(it, carry):
        slot = lax.rem(it, 2)
        row_finish()
        for chunk in range(chunks):
            levels = []
            for j in range(0, CHUNK, 2):
                levels += col_blocks([chunk * CHUNK + j, chunk * CHUNK + j + 1])
            parts[slot, chunk, me] = jnp.concatenate(levels, axis=0)
            for step in range(1, peers):
                ex_copy(slot, chunk, step).start()
        for chunk in range(chunks):
            for step in range(1, peers):
                ex_arrived(slot, chunk, step)
            peak, total = peak_total(parts[slot, chunk])
            level = -relaxed * (peak + jnp.log2(total))
            for j in range(CHUNK):
                g_scaled[chunk * CHUNK + j] = (
                    jnp.broadcast_to(level[j:j + 1, :], (8, LANES)) + log_b[chunk * CHUNK + j]
                )
            row_chunk(chunk)
        for chunk in range(chunks):
            for step in range(1, peers):
                ex_copy(slot, chunk, step).wait_send()
        return carry

    lax.fori_loop(0, ITERS, iteration, 0)

    back = entropic * math.log(2.0)
    for k in range(rows // LANES):
        at = slice(k * LANES, (k + 1) * LANES)
        turned = ((f_scaled[at, :] - log_a[at, :]) * back).T
        f_parts[share, k:k + 1, :] = turned[0:1, :]

    def f_copy(turn):
        return pltpu.make_async_remote_copy(
            src_ref=f_parts.at[share], dst_ref=f_parts.at[share],
            send_sem=f_send.at[turn], recv_sem=f_recv.at[share],
            device_id=share_of(turn), device_id_type=MESH,
        )

    for turn in range(1, shares):
        f_copy(turn).start()
    for k in range(per):
        at = (c_id * R + r_id) * per + k
        g_ref[k:k + 1, :] = ((g_scaled[at] - log_b[at]) * back)[0:1, :]

    def own_scores(block):
        return scores[block, rows:rows + own, :].reshape(own // 8, 8, LANES) + g_scaled[block][None]

    def own_peak(block, peak):
        return jnp.maximum(peak, own_scores(block))

    peak = lax.fori_loop(1, blocks, own_peak, own_scores(0), unroll=5)
    top = jnp.max(peak, axis=2, keepdims=True)
    for step in range(C):
        for turn in range(R):
            if step or turn:
                ft_arrived(col_of(step), rep_of(turn))

    def across(left, right):
        return lax.dot_general(
            left, right, (((1,), (1,)), ((), ())), preferred_element_type=jnp.float32
        )

    def fate_block(block, carry):
        total, weighted = carry
        pieces = [jnp.exp2(own_scores(block * per + k) - top) for k in range(per)]
        total = total + sum(pieces)
        weights = jnp.concatenate([p.reshape(own, LANES) for p in pieces], axis=1)
        high, low = [p.astype(jnp.bfloat16) for p in split(weights, 2)]
        panel = [p.astype(jnp.bfloat16) for p in split(ft[block // R, lax.rem(block, R)], 2)]
        return total, weighted + across(high, jnp.concatenate(panel, axis=0)) + across(
            low, jnp.concatenate([panel[0], jnp.zeros_like(panel[0])], axis=0)
        )

    total, weighted = lax.fori_loop(
        0, C * R, fate_block,
        (jnp.zeros((own // 8, 8, LANES), jnp.float32), jnp.zeros((own, 2 * fates), jnp.float32)),
    )
    weighted = weighted / jnp.sum(total.reshape(own, LANES), axis=1, keepdims=True)
    turned = weighted.T
    out_ref[...] = turned[:fates] + turned[fates:]
    for turn in range(1, shares):
        other = lax.rem(share + turn, shares)
        pltpu.make_async_remote_copy(
            src_ref=f_parts.at[other], dst_ref=f_parts.at[other],
            send_sem=f_send.at[0], recv_sem=f_recv.at[other],
            device_id=share_of(turn), device_id_type=MESH,
        ).wait_recv()
    f_ref[...] = f_parts[...]

    for turn in range(1, shares):
        f_copy(turn).wait_send()
    for turn in range(1, R):
        for step in range(C):
            fwd_copy(col_of(step), turn).wait_send()
    for step in range(1, C):
        tt_copy(step).wait_send()
    for step in range(C):
        for turn in range(R):
            if step or turn:
                ft_copy(step, turn).wait_send()


def solution(mesh):
    X, C, R = mesh.shape["rows"], mesh.shape["cols"], mesh.shape["rep"]

    def body(sources, source_mass, targets, target_mass, fate_panel):
        src_count, dim = sources.shape
        tgt_count, fates = fate_panel.shape
        shares = PAIR * R
        rows, own = src_count // shares, src_count // (C * R)
        blocks = C * R * tgt_count // LANES
        chunks = blocks // CHUNK
        peers = X * shares
        vmem = pl.BlockSpec(memory_space=pltpu.VMEM)
        dma = pltpu.SemaphoreType.DMA
        f32 = jnp.float32
        f_pot, g_pot, fate_rows = pl.pallas_call(
            functools.partial(kernel, (X, C, R, src_count, tgt_count, dim, fates)),
            out_shape=(
                jax.ShapeDtypeStruct((shares, rows // LANES, LANES), f32),
                jax.ShapeDtypeStruct((tgt_count // LANES, LANES), f32),
                jax.ShapeDtypeStruct((fates, own), f32),
            ),
            in_specs=[vmem] * 5,
            out_specs=(vmem,) * 3,
            scratch_shapes=[
                pltpu.VMEM((C, R, dim + 8, tgt_count), f32),
                pltpu.VMEM((C, R, fates, tgt_count), f32),
                pltpu.VMEM((blocks, rows + own, LANES), f32),
                pltpu.VMEM((blocks, 8, LANES), f32),
                pltpu.VMEM((blocks, 8, LANES), f32),
                pltpu.VMEM((rows, LANES), f32),
                pltpu.VMEM((rows, LANES), f32),
                pltpu.VMEM((chunks, rows, LANES), f32),
                pltpu.VMEM((chunks, rows, LANES), f32),
                pltpu.VMEM((2, chunks, peers, CHUNK, LANES), f32),
                pltpu.VMEM((shares, rows // LANES, LANES), f32),
                pltpu.VMEM((rows + own, 6 * dim), jnp.bfloat16),
                pltpu.VMEM((rows + own, LANES), f32),
                pltpu.VMEM((src_count, dim), f32),
                dma((C,)), dma((C,)),
                dma((C, R)), dma((C, R)),
                dma((C, R)), dma((C, R)),
                dma((2, chunks, peers)), dma((2, chunks, peers)),
                dma((shares,)), dma((shares,)),
            ],
            compiler_params=pltpu.CompilerParams(
                collective_id=0, has_side_effects=True, vmem_limit_bytes=48 * 2**20
            ),
            name="transport",
        )(
            sources.T,
            source_mass.reshape(shares, rows // LANES, LANES),
            targets.T,
            target_mass.reshape(1, tgt_count),
            fate_panel.T,
        )
        return f_pot.reshape(src_count), g_pot.reshape(tgt_count), fate_rows.T

    in_specs = (
        P(("parts", "rows"), None),
        P(("parts", "rows")),
        P(("parts", "cols", "rep"), None),
        P(("parts", "cols", "rep")),
        P(("parts", "cols", "rep"), None),
    )
    out_specs = (
        P(("parts", "rows")),
        P(("parts", "cols", "rep")),
        P(("parts", "rows", "cols", "rep"), None),
    )
    return jax.shard_map(body, mesh=mesh, in_specs=in_specs, out_specs=out_specs, check_vma=False)
```

```python
import functools
import math

import jax
import jax.numpy as jnp
from jax import lax
from jax.experimental import pallas as pl
from jax.experimental.pallas import tpu as pltpu
from jax.sharding import PartitionSpec as P

ITERS = 8
LANES = 128
PAIR = 1
CHUNK = 8
entropic = 0.1
relaxed = 1.0 / 1.1
MESH = pl.DeviceIdType.MESH


def split(x, pieces):
    out = []
    for k in range(pieces):
        out.append(x.astype(jnp.bfloat16).astype(jnp.float32))
        x = x - out[-1]
    return out


def peak_total(x):
    peak = jnp.max(x, axis=0)
    return peak, jnp.sum(jnp.exp2(x - peak[None]), axis=0)


def kernel(
    sizes, src_hbm, smass_hbm, tgt_hbm, tmass_hbm, fate_hbm,
    f_ref, g_ref, out_ref,
    tt, ft, scores, log_b, g_scaled, log_a, f_scaled, row_peak, row_total, parts, f_parts,
    lhs, src_level, src_rows, src_ref, smass_ref, tmass_ref, in_sem,
    tt_send, tt_recv, fwd_send, fwd_recv, ft_send, ft_recv, ex_send, ex_recv, f_send, f_recv,
):
    X, C, R, src_count, tgt_count, dim, fates = sizes
    rows = src_count // (R * PAIR)
    own = src_count // (C * R)
    blocks = C * R * tgt_count // LANES
    chunks = blocks // CHUNK
    per = tgt_count // LANES
    width = CHUNK // (R * per)
    groups = rows // 8
    peers = X * PAIR * R
    x_id, c_id, r_id = lax.axis_index("rows"), lax.axis_index("cols"), lax.axis_index("rep")
    c_base = c_id // PAIR * PAIR
    shares = PAIR * R
    share = (c_id - c_base) * R + r_id
    me = x_id * shares + share
    all_sources, all_targets = src_count * X, tgt_count * C * R
    unit = math.log2(math.e) / (dim * entropic)

    def peer(step):
        other = lax.rem(me + step, peers)
        return {
            "rows": other // shares,
            "cols": c_base + lax.rem(other, shares) // R,
            "rep": lax.rem(other, R),
        }

    def share_of(step):
        other = lax.rem(share + step, shares)
        return {"cols": c_base + other // R, "rep": lax.rem(other, R)}

    def col_of(step):
        return lax.rem(c_id + step, C)

    def rep_of(step):
        return lax.rem(r_id + step, R)

    loads = [
        pltpu.make_async_copy(origin, target, in_sem.at[k])
        for k, (origin, target) in enumerate([
            (tgt_hbm, tt.at[c_id, r_id, pl.ds(0, dim)]),
            (tmass_hbm, tmass_ref),
            (src_hbm, src_ref),
            (smass_hbm, smass_ref),
            (fate_hbm, ft.at[c_id, r_id]),
        ])
    ]
    for load in loads:
        load.start()
    barrier = pltpu.get_barrier_semaphore()
    for step in range(1, peers):
        pl.semaphore_signal(barrier, inc=1, device_id=peer(step), device_id_type=MESH)
    for step in range(C):
        for turn in range(R):
            if step or turn:
                pl.semaphore_signal(
                    barrier, inc=1, device_id={"cols": col_of(step), "rep": rep_of(turn)},
                    device_id_type=MESH,
                )

    loads[1].wait()
    tt[c_id, r_id, dim:dim + 8, :] = jnp.broadcast_to(
        jnp.log2(tmass_ref[...] / all_targets), (8, tgt_count)
    )

    loads[0].wait()
    pl.semaphore_wait(barrier, peers - 1 + C * R - 1)

    def tt_copy(step):
        return pltpu.make_async_remote_copy(
            src_ref=tt.at[c_id, r_id], dst_ref=tt.at[c_id, r_id],
            send_sem=tt_send.at[step], recv_sem=tt_recv.at[c_id],
            device_id={"cols": col_of(step)}, device_id_type=MESH,
        )

    def fwd_copy(col, turn):
        return pltpu.make_async_remote_copy(
            src_ref=tt.at[col, r_id], dst_ref=tt.at[col, r_id],
            send_sem=fwd_send.at[col, turn], recv_sem=fwd_recv.at[col, r_id],
            device_id={"rep": rep_of(turn)}, device_id_type=MESH,
        )

    def ft_copy(step, turn):
        return pltpu.make_async_remote_copy(
            src_ref=ft.at[c_id, r_id], dst_ref=ft.at[c_id, r_id],
            send_sem=ft_send.at[step, turn], recv_sem=ft_recv.at[c_id, r_id],
            device_id={"cols": col_of(step), "rep": rep_of(turn)}, device_id_type=MESH,
        )

    def tt_arrived(col):
        pltpu.make_async_remote_copy(
            src_ref=tt.at[col, r_id], dst_ref=tt.at[col, r_id],
            send_sem=tt_send.at[0], recv_sem=tt_recv.at[col],
            device_id={"cols": col}, device_id_type=MESH,
        ).wait_recv()

    def fwd_arrived(col, rep):
        pltpu.make_async_remote_copy(
            src_ref=tt.at[col, rep], dst_ref=tt.at[col, rep],
            send_sem=fwd_send.at[col, 0], recv_sem=fwd_recv.at[col, rep],
            device_id={"rep": rep}, device_id_type=MESH,
        ).wait_recv()

    def ft_arrived(col, rep):
        pltpu.make_async_remote_copy(
            src_ref=ft.at[col, rep], dst_ref=ft.at[col, rep],
            send_sem=ft_send.at[0, 0], recv_sem=ft_recv.at[col, rep],
            device_id={"cols": col, "rep": rep}, device_id_type=MESH,
        ).wait_recv()

    for step in range(1, C):
        tt_copy(step).start()
    for turn in range(1, R):
        fwd_copy(c_id, turn).start()
    loads[2].wait()
    for k in range(src_count // LANES):
        at = slice(k * LANES, (k + 1) * LANES)
        src_rows[at, :] = src_ref[:, at].T
    first = pl.multiple_of(share * rows, rows)
    first_own = pl.multiple_of((c_id * R + r_id) * own, own)
    mine = jnp.concatenate(
        [src_rows[pl.ds(first, rows), :], src_rows[pl.ds(first_own, own), :]], axis=0
    )
    src_level[...] = jnp.broadcast_to(
        jnp.sum(mine * mine, axis=1, keepdims=True) * unit, src_level.shape
    )
    a, b, c = split(mine * (2.0 * unit), 3)
    lhs[...] = jnp.concatenate([a, a, b, a, c, b], axis=1).astype(jnp.bfloat16)


    def fill(col, rep):
        block = tt[col, rep, 0:dim, :]
        a, b, c = [p.astype(jnp.bfloat16) for p in split(block, 3)]
        rhs = jnp.concatenate([a, b, a, c, a, b], axis=0)
        products = jnp.dot(lhs[...], rhs, preferred_element_type=jnp.float32)
        tgt_level = jnp.sum(block * block, axis=0, keepdims=True) * unit
        for k in range(per):
            at = (col * R + rep) * per + k
            lanes = slice(k * LANES, (k + 1) * LANES)
            scores[at] = products[:, lanes] - (src_level[...] + tgt_level[:, lanes])
            level = tt[col, rep, dim:dim + 8, k * LANES:(k + 1) * LANES]
            log_b[at] = level
            g_scaled[at] = level

    def row_chunk(chunk):
        base = chunk * CHUNK
        g_chunk = g_scaled[pl.ds(base, CHUNK)]

        def row_group(group, carry):
            at = pl.multiple_of(group * 8, 8)
            x = scores[pl.ds(base, CHUNK), pl.ds(at, 8), :] + g_chunk
            peak, total = peak_total(x)
            row_peak[chunk, pl.ds(at, 8), :] = peak
            row_total[chunk, pl.ds(at, 8), :] = total
            return carry

        lax.fori_loop(0, groups, row_group, 0, unroll=8)

    def row_finish():
        peaks = row_peak[...]
        top = jnp.max(jnp.max(peaks, axis=0), axis=1, keepdims=True)
        totals = jnp.sum(row_total[...] * jnp.exp2(peaks - top[None]), axis=0)
        level = top + jnp.log2(jnp.sum(totals, axis=1, keepdims=True))
        f_scaled[...] = log_a[...] - relaxed * level

    def col_blocks(blocks):
        peaks, totals = [[] for b in blocks], [[] for b in blocks]
        for q in range(rows // LANES):
            at = slice(q * LANES, (q + 1) * LANES)
            f_rows = f_scaled[at, :]
            for k, block in enumerate(blocks):
                x = (scores[block, at, :] + f_rows).reshape(LANES // 8, 8, LANES)
                peak, total = peak_total(x)
                peaks[k].append(peak)
                totals[k].append(total)
        for k in range(len(blocks)):
            top = jnp.max(functools.reduce(jnp.maximum, peaks[k]), axis=0, keepdims=True)
            whole = sum(t * jnp.exp2(p - top) for p, t in zip(peaks[k], totals[k]))
            yield top + jnp.log2(jnp.sum(whole, axis=0, keepdims=True))

    def ex_copy(slot, chunk, step):
        return pltpu.make_async_remote_copy(
            src_ref=parts.at[slot, chunk, me], dst_ref=parts.at[slot, chunk, me],
            send_sem=ex_send.at[slot, chunk, step], recv_sem=ex_recv.at[slot, chunk, me],
            device_id=peer(step), device_id_type=MESH,
        )

    def ex_arrived(slot, chunk, step):
        other = lax.rem(me + step, peers)
        pltpu.make_async_remote_copy(
            src_ref=parts.at[slot, chunk, other], dst_ref=parts.at[slot, chunk, other],
            send_sem=ex_send.at[slot, chunk, 0], recv_sem=ex_recv.at[slot, chunk, other],
            device_id=peer(step), device_id_type=MESH,
        ).wait_recv()

    fill(c_id, r_id)
    loads[3].wait()
    for k in range(rows // LANES):
        level = jnp.log2(smass_ref[share, k:k + 1, :] / all_sources)
        log_a[k * LANES:(k + 1) * LANES, :] = jnp.broadcast_to(level, (LANES, LANES)).T
    for turn in range(1, R):
        fwd_arrived(c_id, rep_of(turn))
        fill(c_id, rep_of(turn))
    ready = None
    for p in range(chunks):
        chunk = lax.rem(c_id // width + p, chunks)
        if p:
            cols = [chunk * width + k for k in range(width)]
        else:
            cols = [chunk * width + lax.rem(c_id + k, width) for k in range(1, width)]
        for col in cols:
            tt_arrived(col)
            for turn in range(1, R):
                fwd_copy(col, turn).start()
            fill(col, r_id)
        if ready is not None:
            row_chunk(ready)
        for col in cols:
            for turn in range(1, R):
                fwd_arrived(col, rep_of(turn))
                fill(col, rep_of(turn))
        ready = chunk
    loads[4].wait()
    for step in list(range(1, C)) + [0]:
        for turn in range(R):
            if step or turn:
                ft_copy(step, turn).start()
    row_chunk(ready)

    def iteration(it, carry):
        slot = lax.rem(it, 2)
        row_finish()
        for chunk in range(chunks):
            levels = []
            for j in range(0, CHUNK, 2):
                levels += col_blocks([chunk * CHUNK + j, chunk * CHUNK + j + 1])
            parts[slot, chunk, me] = jnp.concatenate(levels, axis=0)
            for step in range(1, peers):
                ex_copy(slot, chunk, step).start()
        for chunk in range(chunks):
            for step in range(1, peers):
                ex_arrived(slot, chunk, step)
            peak, total = peak_total(parts[slot, chunk])
            level = -relaxed * (peak + jnp.log2(total))
            for j in range(CHUNK):
                g_scaled[chunk * CHUNK + j] = (
                    jnp.broadcast_to(level[j:j + 1, :], (8, LANES)) + log_b[chunk * CHUNK + j]
                )
            row_chunk(chunk)
        for chunk in range(chunks):
            for step in range(1, peers):
                ex_copy(slot, chunk, step).wait_send()
        return carry

    lax.fori_loop(0, ITERS, iteration, 0)

    back = entropic * math.log(2.0)
    for k in range(rows // LANES):
        at = slice(k * LANES, (k + 1) * LANES)
        turned = ((f_scaled[at, :] - log_a[at, :]) * back).T
        f_parts[share, k:k + 1, :] = turned[0:1, :]

    def f_copy(turn):
        return pltpu.make_async_remote_copy(
            src_ref=f_parts.at[share], dst_ref=f_parts.at[share],
            send_sem=f_send.at[turn], recv_sem=f_recv.at[share],
            device_id=share_of(turn), device_id_type=MESH,
        )

    for turn in range(1, shares):
        f_copy(turn).start()
    for k in range(per):
        at = (c_id * R + r_id) * per + k
        g_ref[k:k + 1, :] = ((g_scaled[at] - log_b[at]) * back)[0:1, :]

    def own_scores(block):
        return scores[block, rows:rows + own, :].reshape(own // 8, 8, LANES) + g_scaled[block][None]

    def own_peak(block, peak):
        return jnp.maximum(peak, own_scores(block))

    peak = lax.fori_loop(1, blocks, own_peak, own_scores(0), unroll=5)
    top = jnp.max(peak, axis=2, keepdims=True)
    for step in range(C):
        for turn in range(R):
            if step or turn:
                ft_arrived(col_of(step), rep_of(turn))

    def across(left, right):
        return lax.dot_general(
            left, right, (((1,), (1,)), ((), ())), preferred_element_type=jnp.float32
        )

    def fate_block(block, carry):
        total, weighted = carry
        pieces = [jnp.exp2(own_scores(block * per + k) - top) for k in range(per)]
        total = total + sum(pieces)
        weights = jnp.concatenate([p.reshape(own, LANES) for p in pieces], axis=1)
        high, low = [p.astype(jnp.bfloat16) for p in split(weights, 2)]
        panel = [p.astype(jnp.bfloat16) for p in split(ft[block // R, lax.rem(block, R)], 2)]
        return total, weighted + across(high, jnp.concatenate(panel, axis=0)) + across(
            low, jnp.concatenate([panel[0], jnp.zeros_like(panel[0])], axis=0)
        )

    total, weighted = lax.fori_loop(
        0, C * R, fate_block,
        (jnp.zeros((own // 8, 8, LANES), jnp.float32), jnp.zeros((own, 2 * fates), jnp.float32)),
    )
    weighted = weighted / jnp.sum(total.reshape(own, LANES), axis=1, keepdims=True)
    turned = weighted.T
    out_ref[...] = turned[:fates] + turned[fates:]
    for turn in range(1, shares):
        other = lax.rem(share + turn, shares)
        pltpu.make_async_remote_copy(
            src_ref=f_parts.at[other], dst_ref=f_parts.at[other],
            send_sem=f_send.at[0], recv_sem=f_recv.at[other],
            device_id=share_of(turn), device_id_type=MESH,
        ).wait_recv()
    f_ref[...] = f_parts[...]

    for turn in range(1, shares):
        f_copy(turn).wait_send()
    for turn in range(1, R):
        for step in range(C):
            fwd_copy(col_of(step), turn).wait_send()
    for step in range(1, C):
        tt_copy(step).wait_send()
    for step in range(C):
        for turn in range(R):
            if step or turn:
                ft_copy(step, turn).wait_send()


def solution(mesh):
    X, C, R = mesh.shape["rows"], mesh.shape["cols"], mesh.shape["rep"]

    def body(sources, source_mass, targets, target_mass, fate_panel):
        src_count, dim = sources.shape
        tgt_count, fates = fate_panel.shape
        shares = PAIR * R
        rows, own = src_count // shares, src_count // (C * R)
        blocks = C * R * tgt_count // LANES
        chunks = blocks // CHUNK
        peers = X * shares
        vmem = pl.BlockSpec(memory_space=pltpu.VMEM)
        dma = pltpu.SemaphoreType.DMA
        f32 = jnp.float32
        f_pot, g_pot, fate_rows = pl.pallas_call(
            functools.partial(kernel, (X, C, R, src_count, tgt_count, dim, fates)),
            out_shape=(
                jax.ShapeDtypeStruct((shares, rows // LANES, LANES), f32),
                jax.ShapeDtypeStruct((tgt_count // LANES, LANES), f32),
                jax.ShapeDtypeStruct((fates, own), f32),
            ),
            in_specs=[pl.BlockSpec(memory_space=pltpu.HBM)] * 5,
            out_specs=(vmem,) * 3,
            scratch_shapes=[
                pltpu.VMEM((C, R, dim + 8, tgt_count), f32),
                pltpu.VMEM((C, R, fates, tgt_count), f32),
                pltpu.VMEM((blocks, rows + own, LANES), f32),
                pltpu.VMEM((blocks, 8, LANES), f32),
                pltpu.VMEM((blocks, 8, LANES), f32),
                pltpu.VMEM((rows, LANES), f32),
                pltpu.VMEM((rows, LANES), f32),
                pltpu.VMEM((chunks, rows, LANES), f32),
                pltpu.VMEM((chunks, rows, LANES), f32),
                pltpu.VMEM((2, chunks, peers, CHUNK, LANES), f32),
                pltpu.VMEM((shares, rows // LANES, LANES), f32),
                pltpu.VMEM((rows + own, 6 * dim), jnp.bfloat16),
                pltpu.VMEM((rows + own, LANES), f32),
                pltpu.VMEM((src_count, dim), f32),
                pltpu.VMEM((dim, src_count), f32),
                pltpu.VMEM((shares, rows // LANES, LANES), f32),
                pltpu.VMEM((1, tgt_count), f32),
                dma((5,)),
                dma((C,)), dma((C,)),
                dma((C, R)), dma((C, R)),
                dma((C, R)), dma((C, R)),
                dma((2, chunks, peers)), dma((2, chunks, peers)),
                dma((shares,)), dma((shares,)),
            ],
            compiler_params=pltpu.CompilerParams(
                collective_id=0, has_side_effects=True, vmem_limit_bytes=48 * 2**20
            ),
            name="transport",
        )(
            sources.T,
            source_mass.reshape(shares, rows // LANES, LANES),
            targets.T,
            target_mass.reshape(1, tgt_count),
            fate_panel.T,
        )
        return f_pot.reshape(src_count), g_pot.reshape(tgt_count), fate_rows.T

    in_specs = (
        P(("parts", "rows"), None),
        P(("parts", "rows")),
        P(("parts", "cols", "rep"), None),
        P(("parts", "cols", "rep")),
        P(("parts", "cols", "rep"), None),
    )
    out_specs = (
        P(("parts", "rows")),
        P(("parts", "cols", "rep")),
        P(("parts", "rows", "cols", "rep"), None),
    )
    return jax.shard_map(body, mesh=mesh, in_specs=in_specs, out_specs=out_specs, check_vma=False)
```
